128 devices in a mesh: row: 4 (over y), col: 4 (over x_hi, core), en: 8 (over x_lo, z).
Axes of the slice: x: 4 (x_hi: 2, x_lo: 2; x = x_hi * 2 + x_lo), y: 4, z: 4, core: 2. Of those that a mesh axis runs over, the one named last changes fastest.
Arguments:
- lesser: bfloat16 [2, 4, 3, 128, 512, 128], P(None, 'row', None, 'col', 'en'), may hold values from -6 to 6
- greater: bfloat16 [2, 4, 3, 128, 512, 128], P(None, 'row', None, 'col', 'en'), may hold values from -6 to 6
- coupling: bfloat16 [4, 3, 128, 128], replicated, may hold values from -0.3125 to 0.3125
Outputs:
- screened: bfloat16 [2, 4, 5, 128, 512, 128], P(None, 'row', None, None, ('col', 'en'))
The draws below stay inside these ranges and needn't reach their ends.
All inputs are finite; a program needn't handle non-finite values.
Results may differ from the reference program's by a relative error of at most 0.025.
Values may be sent and summed in bfloat16 or wider, within the bound.
A program may use at most 128 MiB of HBM per device.

```python
import math
import jax
import jax.numpy as jnp
from jax import lax

TILE = 128
NE = 512
BAND = 3
NT = 4


def level_of(key, dims, shards, smallest, high):
    level, own = 1.0, jax.random.fold_in(key, 6)
    for position, blocks in shards:
        draws = jnp.exp(jax.random.uniform(jax.random.fold_in(own, position), (blocks,), jnp.float32, smallest / len(shards), high / len(shards)))
        level = level * jnp.repeat(draws, dims[position] // blocks).reshape([-1 if axis == position else 1 for axis in range(len(dims))])
    return level


def noise(rng, extent, spread, reach, split=(), dtype=jnp.bfloat16):
    values = spread * jax.random.normal(rng, extent, jnp.float32)
    if split:
        values = values * level_of(rng, extent, split, -0.22, 0.18)
    return jnp.clip(values, -reach, reach).astype(dtype)


def setup_inputs(seed: int = 0) -> dict:
    key_list = jax.random.split(jax.random.key(seed), 4)
    return {
        "lesser": noise(key_list[0], (2, NT, BAND, TILE, NE, TILE), 1.0, 6.0, ((1, 4), (3, 4), (4, 8))),
        "greater": noise(key_list[1], (2, NT, BAND, TILE, NE, TILE), 1.0, 6.0, ((1, 4), (3, 4), (4, 8))),
        "coupling": noise(key_list[2], (NT, BAND, TILE, TILE), (BAND * TILE) ** -0.5, 0.3125),
    }


def keep_rounded(values):
    return lax.optimization_barrier(values.astype(jnp.bfloat16)).astype(jnp.float32)

def correlate_pair(less_tile, great_tile):
    length = 2 * NE
    first = lax.complex(less_tile[0].astype(jnp.float32), less_tile[1].astype(jnp.float32))
    flipped = jnp.transpose(great_tile, (0, 3, 2, 1))
    second = lax.complex(flipped[0].astype(jnp.float32), flipped[1].astype(jnp.float32))
    spec_one = jnp.fft.fft(first, n=length, axis=1)
    spec_two = jnp.fft.ifft(second, n=length, axis=1) * length
    one_re = keep_rounded(spec_one.real)
    one_im = keep_rounded(spec_one.imag)
    two_re = keep_rounded(spec_two.real)
    two_im = keep_rounded(spec_two.imag)
    prod_re = keep_rounded(one_re * two_re - one_im * two_im)
    prod_im = keep_rounded(one_re * two_im + one_im * two_re)
    lagged = jnp.fft.ifft(lax.complex(prod_re, prod_im), axis=1)
    lagged = jnp.concatenate([lagged[:, length - NE // 2:], lagged[:, :NE // 2]], axis=1)
    scale = 1.0 / math.sqrt(length)
    return jnp.stack([scale * lagged.imag, -scale * lagged.real]).astype(jnp.bfloat16)

def reference(lesser, greater, coupling):
    halves = {}
    for first in range(NT):
        polar = {}
        for slot in range(3):
            partner = first + slot - 1
            if 0 <= partner < NT:
                polar[slot] = correlate_pair(lesser[:, first, slot], greater[:, partner, 2 - slot])
        for band in range(5):
            total = jnp.zeros((2, TILE, NE, TILE), jnp.float32)
            column = first + band - 2
            for slot in range(3):
                offset = band - slot
                partner = first + slot - 1
                if 0 <= offset <= 2 and 0 <= column < NT and (0 <= partner < NT):
                    slab = polar[slot].astype(jnp.float32)
                    tile = coupling[column, 2 - offset].astype(jnp.float32)
                    total = total + keep_rounded(jnp.einsum('xaln,mn->xalm', slab, tile))
            halves[first, band] = total.astype(jnp.bfloat16)
    rows = []
    for target in range(NT):
        slots = []
        for band in range(5):
            total = jnp.zeros((2, TILE, NE, TILE), jnp.float32)
            for source in (target - 1, target, target + 1):
                inner = band + target - source
                if 0 <= source < NT and 0 <= inner <= 4:
                    tile = coupling[target, source - target + 1].astype(jnp.float32)
                    slab = halves[source, inner].astype(jnp.float32)
                    total = total + keep_rounded(jnp.einsum('mk,xkln->xmln', tile, slab))
            slots.append(total.astype(jnp.bfloat16))
        rows.append(jnp.stack(slots, axis=1))
    return jnp.stack(rows, axis=1)
```

```python
import math

import jax
import jax.numpy as jnp
import ml_dtypes
import numpy as np
from jax import lax
from jax.experimental import pallas as pl
from jax.experimental.pallas import tpu as pltpu
from jax.sharding import PartitionSpec as P

MESH = pl.DeviceIdType.MESH
ORDER = (1, 0, 2)
FREQ = 384
LENGTH = 2 * FREQ


def tables(energies):
    freq = 2 * np.arange(FREQ)[:, None] + 1
    ahead = freq * np.arange(energies)[None, :] % (2 * LENGTH)
    back = (np.arange(energies) - energies // 2)[:, None] * freq.T % (2 * LENGTH)
    ahead = ahead * (math.pi / LENGTH)
    back = back * (math.pi / LENGTH)
    forward = np.concatenate([np.cos(ahead), np.sin(ahead)], axis=0)
    inverse = np.concatenate([np.cos(back), np.sin(back)], axis=1)
    return forward.astype(ml_dtypes.bfloat16), inverse.astype(ml_dtypes.bfloat16)


def kernel(
    lesser,
    greater,
    coupling,
    forward_hbm,
    inverse_hbm,
    out,
    forward,
    inverse,
    graw,
    turned,
    xin,
    yin,
    pout,
    own,
    near,
    total,
    swap,
    wide,
    left,
    right,
    xcat,
    ycat,
    spec_one,
    spec_two,
    product,
    staged,
    sem_local,
    sem_raw,
    sem_x,
    sem_y,
    sem_p,
    sem_n,
    sem_out,
):
    row = lax.axis_index("row")
    col = lax.axis_index("col")
    en = lax.axis_index("en")
    me = col * 8 + en
    below, above = lax.rem(row + 3, 4), lax.rem(row + 1, 4)

    def peer(step):
        index = lax.rem(me + step, 32)
        return index, (row, index // 8, lax.rem(index, 8))

    def local(src, dst, index):
        return pltpu.make_async_copy(src, dst, sem_local.at[index])

    barrier = pltpu.get_barrier_semaphore()

    def greet(step, carry):
        pl.semaphore_signal(barrier, inc=1, device_id=peer(step)[1], device_id_type=MESH)
        return carry

    load_raw = local(greater.at[:, 0, 1], graw.at[1], 0)
    load_raw.start()
    load_forward = local(forward_hbm, forward, 1)
    load_forward.start()
    load_inverse = local(inverse_hbm, inverse, 2)
    load_inverse.start()
    lax.fori_loop(1, 32, greet, 0)
    pl.semaphore_signal(barrier, inc=1, device_id=(below, col, en), device_id_type=MESH)
    pl.semaphore_signal(barrier, inc=1, device_id=(above, col, en), device_id_type=MESH)
    pl.semaphore_wait(barrier, 33)

    raw_down = pltpu.make_async_remote_copy(
        src_ref=greater.at[:, 0, 0],
        dst_ref=graw.at[2],
        send_sem=sem_raw.at[0],
        recv_sem=sem_raw.at[1],
        device_id=(below, col, en),
        device_id_type=MESH,
    )
    raw_up = pltpu.make_async_remote_copy(
        src_ref=greater.at[:, 0, 2],
        dst_ref=graw.at[0],
        send_sem=sem_raw.at[2],
        recv_sem=sem_raw.at[3],
        device_id=(above, col, en),
        device_id_type=MESH,
    )
    raw_down.start()
    raw_up.start()

    def send_x(slot):
        def body(step, carry):
            to = lax.rem(en + step, 8)
            pltpu.make_async_remote_copy(
                src_ref=lesser.at[:, 0, slot, pl.ds(4 * to, 4)],
                dst_ref=xin.at[slot, :, :, pl.ds(64 * en, 64), :],
                send_sem=sem_x.at[0, slot],
                recv_sem=sem_x.at[1, slot],
                device_id=(row, col, to),
                device_id_type=MESH,
            ).start()
            return carry

        lax.fori_loop(1, 8, body, 0)
        keep = local(
            lesser.at[:, 0, slot, pl.ds(4 * en, 4)],
            xin.at[slot, :, :, pl.ds(64 * en, 64), :],
            3 + slot,
        )
        keep.start()
        return keep

    def send_y(slot):
        def body(step, carry):
            index, target = peer(step)
            pltpu.make_async_remote_copy(
                src_ref=turned.at[slot, :, pl.ds(64 * index, 64), :],
                dst_ref=yin.at[slot, me],
                send_sem=sem_y.at[0, slot],
                recv_sem=sem_y.at[1, slot],
                device_id=target,
                device_id_type=MESH,
            ).start()
            return carry

        lax.fori_loop(1, 32, body, 0)
        keep = local(turned.at[slot, :, pl.ds(64 * me, 64), :], yin.at[slot, me], 6 + slot)
        keep.start()
        return keep

    def send_p(slot):
        def body(step, carry):
            index, target = peer(step)
            pltpu.make_async_remote_copy(
                src_ref=pout.at[slot, :, :, pl.ds(16 * index, 16), :],
                dst_ref=own.at[slot, :, pl.ds(4 * me, 4)],
                send_sem=sem_p.at[0, slot],
                recv_sem=sem_p.at[1, slot],
                device_id=target,
                device_id_type=MESH,
            ).start()
            return carry

        lax.fori_loop(1, 32, body, 0)
        keep = local(
            pout.at[slot, :, :, pl.ds(16 * me, 16), :],
            own.at[slot, :, pl.ds(4 * me, 4)],
            9 + slot,
        )
        keep.start()
        return keep

    def send_n(slot):
        copies = []
        for side, target in ((0, above), (1, below)):
            copy = pltpu.make_async_remote_copy(
                src_ref=own.at[slot],
                dst_ref=near.at[side, slot],
                send_sem=sem_n.at[0, side, slot],
                recv_sem=sem_n.at[1, side, slot],
                device_id=(target, col, en),
                device_id_type=MESH,
            )
            copy.start()
            copies.append(copy)
        return copies

    def bytes_of(ref, sem):
        pltpu.make_async_copy(ref, ref, sem).wait()

    def turn(slot):
        def part(p, carry):
            def one(s, inner):
                low = graw[slot, p, s]
                high = graw[slot, p, s + 16]
                square = jnp.concatenate([low, high], axis=0).astype(jnp.float32)
                swap[pl.ds(s, 128, stride=16), :] = square.T
                return inner

            lax.fori_loop(0, 16, one, 0)
            turned[slot, p] = swap[...].astype(jnp.bfloat16)
            return carry

        lax.fori_loop(0, 2, part, 0)

    lane = lax.broadcasted_iota(jnp.int32, (16, 128), 1)

    def correlate(slot):
        def body(a, carry):
            for p in range(2):
                xcat[:, p * 128 : (p + 1) * 128] = xin[slot, p, a]
            for p in range(2):
                for c in range(4):
                    for k in range(4):
                        one = yin[slot, c * 8 + 2 * k, p, pl.ds(16 * a, 16), :].astype(jnp.float32)
                        two = yin[slot, c * 8 + 2 * k + 1, p, pl.ds(16 * a, 16), :].astype(jnp.float32)
                        first = jnp.where(lane < 64, one, pltpu.roll(two, 64, 1))
                        second = jnp.where(lane < 64, pltpu.roll(one, 64, 1), two)
                        base = p * 128 + c * 32
                        ycat[base : base + 16, k * 128 : (k + 1) * 128] = first.astype(jnp.bfloat16)
                        ycat[base + 16 : base + 32, k * 128 : (k + 1) * 128] = second.astype(jnp.bfloat16)
            spec_one[...] = jnp.dot(forward[...], xcat[...], preferred_element_type=jnp.float32)
            spec_two[...] = lax.dot_general(
                forward[...], ycat[...], (((1,), (1,)), ((), ())), preferred_element_type=jnp.float32
            )

            def mix(step, inner):
                cos_rows = pl.ds(step * 16, 16)
                sin_rows = pl.ds(FREQ + step * 16, 16)
                one_rr, one_ri = spec_one[cos_rows, 0:128], spec_one[cos_rows, 128:256]
                one_sr, one_si = spec_one[sin_rows, 0:128], spec_one[sin_rows, 128:256]
                two_rr, two_ri = spec_two[cos_rows, 0:128], spec_two[cos_rows, 128:256]
                two_sr, two_si = spec_two[sin_rows, 0:128], spec_two[sin_rows, 128:256]
                a_re, a_im = one_rr + one_si, one_ri - one_sr
                a_re_m, a_im_m = one_rr - one_si, one_ri + one_sr
                b_re, b_im = two_rr - two_si, two_ri + two_sr
                b_re_m, b_im_m = two_rr + two_si, two_ri - two_sr
                s_re = a_re * b_re - a_im * b_im
                s_im = a_re * b_im + a_im * b_re
                s_re_m = a_re_m * b_re_m - a_im_m * b_im_m
                s_im_m = a_re_m * b_im_m + a_im_m * b_re_m
                product[cos_rows, 0:128] = (s_re + s_re_m).astype(jnp.bfloat16)
                product[sin_rows, 0:128] = (s_im_m - s_im).astype(jnp.bfloat16)
                product[cos_rows, 128:256] = (s_im + s_im_m).astype(jnp.bfloat16)
                product[sin_rows, 128:256] = (s_re - s_re_m).astype(jnp.bfloat16)
                return inner

            lax.fori_loop(0, FREQ // 16, mix, 0)
            lagged = jnp.dot(inverse[...], product[...], preferred_element_type=jnp.float32)
            scale = 1.0 / (LENGTH * 32.0)
            pout[slot, 0, a] = (scale * lagged[:, 128:256]).astype(jnp.bfloat16)
            pout[slot, 1, a] = (-scale * lagged[:, 0:128]).astype(jnp.bfloat16)
            return carry

        lax.fori_loop(0, 4, body, 0)

    def apply_left(tile_of, slot, side):
        column = side + slot

        def part(p, carry):
            swap[...] = tile_of(p).astype(jnp.float32).reshape(2048, 128)
            for pair in range(8):
                both = jnp.concatenate(
                    [
                        swap[pl.ds(2 * pair, 128, stride=16), :],
                        swap[pl.ds(2 * pair + 1, 128, stride=16), :],
                    ],
                    axis=1,
                ).astype(jnp.bfloat16)
                made = jnp.dot(left[side], both, preferred_element_type=jnp.float32)
                lower = pl.ds(256 * pair, 128)
                upper = pl.ds(256 * pair + 128, 128)
                total[p, column, lower, :] += made[:, 0:128]
                total[p, column, upper, :] += made[:, 128:256]
            return carry

        lax.fori_loop(0, 2, part, 0)

    waits = {}
    kept = {}
    kept["x", 1] = send_x(1)
    load_raw.wait()
    turn(1)
    kept["y", 1] = send_y(1)
    kept["x", 0] = send_x(0)
    kept["x", 2] = send_x(2)

    for side in range(3):
        inside = ((row + side - 1 >= 0) & (row + side - 1 < 4)).astype(jnp.float32)
        left[side] = (coupling[row, side].astype(jnp.float32) * inside).astype(jnp.bfloat16)
    for b in range(5):
        for s in range(5):
            block = (slice(b * 128, b * 128 + 128), slice(s * 128, s * 128 + 128))
            if abs(b - s) > 1:
                right[block] = jnp.zeros((128, 128), jnp.bfloat16)
            else:
                tile_b, tile_c = row + b - 2, row + s - 2
                inside = (
                    (tile_b >= 0) & (tile_b < 4) & (tile_c >= 0) & (tile_c < 4)
                ).astype(jnp.float32)
                safe = jnp.clip(tile_c, 0, 3)
                tile = coupling[safe, b - s + 1].astype(jnp.float32) * inside
                right[block] = tile.T.astype(jnp.bfloat16)

    def clear(step, carry):
        for b in range(5):
            total[0, b, pl.ds(step * 256, 256), :] = jnp.zeros((256, 128), jnp.float32)
            total[1, b, pl.ds(step * 256, 256), :] = jnp.zeros((256, 128), jnp.float32)
        return carry

    lax.fori_loop(0, 8, clear, 0)

    raw_up.wait_recv()
    turn(0)
    kept["y", 0] = send_y(0)
    load_forward.wait()
    load_inverse.wait()

    def arrive(slot):
        bytes_of(xin.at[slot, :, :, pl.ds(0, 448), :], sem_x.at[1, slot])
        kept["x", slot].wait()
        bytes_of(yin.at[slot, pl.ds(0, 31)], sem_y.at[1, slot])
        kept["y", slot].wait()

    def gather(slot):
        bytes_of(own.at[slot, :, pl.ds(0, 124)], sem_p.at[1, slot])
        kept["p", slot].wait()

    arrive(1)
    correlate(1)
    kept["p", 1] = send_p(1)
    raw_down.wait_recv()
    turn(2)
    kept["y", 2] = send_y(2)
    gather(1)
    waits[1] = send_n(1)
    apply_left(lambda p: own[1, p], 1, 1)
    arrive(0)
    correlate(0)
    kept["p", 0] = send_p(0)
    gather(0)
    waits[0] = send_n(0)
    apply_left(lambda p: own[0, p], 0, 1)
    arrive(2)
    correlate(2)
    kept["p", 2] = send_p(2)
    for side in range(2):
        waits[1][side].wait_recv()
        apply_left(lambda p: near[side, 1, p], 1, 2 * side)
    gather(2)
    waits[2] = send_n(2)
    apply_left(lambda p: own[2, p], 2, 1)
    for side in range(2):
        waits[0][side].wait_recv()
        apply_left(lambda p: near[side, 0, p], 0, 2 * side)
    for side in range(2):
        waits[2][side].wait_recv()
        apply_left(lambda p: near[side, 2, p], 2, 2 * side)

    for p in range(2):
        def finish(quad, carry):
            rows = pl.ds(quad * 512, 512)
            whole = jnp.concatenate(
                [total[p, b, rows, :].astype(jnp.bfloat16) for b in range(5)], axis=1
            )
            for s in range(5):
                low, high = max(s - 1, 0) * 128, min(s + 2, 5) * 128
                made = jnp.dot(
                    whole[:, low:high],
                    right[low:high, s * 128 : s * 128 + 128],
                    preferred_element_type=jnp.float32,
                )
                for lag in range(4):
                    wide[s, pl.ds(quad * 4 + lag, 128, stride=16), :] = made[lag * 128 : lag * 128 + 128]
            return carry

        lax.fori_loop(0, 4, finish, 0)
        for s in range(5):
            staged[p, s] = wide[s].astype(jnp.bfloat16).reshape(128, 16, 128)
        pltpu.make_async_copy(staged.at[p], out.at[p, 0], sem_out.at[p]).start()

    for p in range(2):
        pltpu.make_async_copy(staged.at[p], out.at[p, 0], sem_out.at[p]).wait()
    raw_down.wait_send()
    raw_up.wait_send()
    for slot in ORDER:
        bytes_of(xin.at[slot, :, :, pl.ds(0, 448), :], sem_x.at[0, slot])
        bytes_of(yin.at[slot, pl.ds(0, 31)], sem_y.at[0, slot])
        bytes_of(own.at[slot, :, pl.ds(0, 124)], sem_p.at[0, slot])
        for copy in waits[slot]:
            copy.wait_send()


def shards(lesser, greater, coupling):
    forward, inverse = tables(512)
    half = jnp.bfloat16
    whole = jnp.float32
    anywhere = pl.BlockSpec(memory_space=pl.ANY)
    return pl.pallas_call(
        kernel,
        out_shape=jax.ShapeDtypeStruct((2, 1, 5, 128, 16, 128), half),
        in_specs=[anywhere, anywhere, pl.BlockSpec(memory_space=pltpu.VMEM), anywhere, anywhere],
        out_specs=anywhere,
        scratch_shapes=[
            pltpu.VMEM((LENGTH, 512), half),
            pltpu.VMEM((512, LENGTH), half),
            pltpu.VMEM((3, 2, 32, 64, 128), half),
            pltpu.VMEM((3, 2, 2048, 128), half),
            pltpu.VMEM((3, 2, 4, 512, 128), half),
            pltpu.VMEM((3, 32, 2, 64, 128), half),
            pltpu.VMEM((3, 2, 4, 512, 128), half),
            pltpu.VMEM((3, 2, 128, 16, 128), half),
            pltpu.VMEM((2, 3, 2, 128, 16, 128), half),
            pltpu.VMEM((2, 5, 2048, 128), whole),
            pltpu.VMEM((2048, 128), whole),
            pltpu.VMEM((5, 2048, 128), whole),
            pltpu.VMEM((3, 128, 128), half),
            pltpu.VMEM((640, 640), half),
            pltpu.VMEM((512, 256), half),
            pltpu.VMEM((256, 512), half),
            pltpu.VMEM((LENGTH, 256), whole),
            pltpu.VMEM((LENGTH, 256), whole),
            pltpu.VMEM((LENGTH, 256), half),
            pltpu.VMEM((2, 5, 128, 16, 128), half),
            pltpu.SemaphoreType.DMA((12,)),
            pltpu.SemaphoreType.DMA((4,)),
            pltpu.SemaphoreType.DMA((2, 3)),
            pltpu.SemaphoreType.DMA((2, 3)),
            pltpu.SemaphoreType.DMA((2, 3)),
            pltpu.SemaphoreType.DMA((2, 2, 3)),
            pltpu.SemaphoreType.DMA((2,)),
        ],
        compiler_params=pltpu.CompilerParams(
            collective_id=0, has_side_effects=True, vmem_limit_bytes=60 * 1024 * 1024
        ),
        cost_estimate=pl.CostEstimate(flops=10**10, bytes_accessed=2 * 10**7, transcendentals=0),
    )(lesser, greater, coupling, jnp.asarray(forward), jnp.asarray(inverse))


def solution(mesh):
    placed = (P(None, "row", None, "col", "en", None), P(None, "row", None, "col", "en", None), P())
    return jax.shard_map(
        shards,
        mesh=mesh,
        in_specs=placed,
        out_specs=P(None, "row", None, None, ("col", "en"), None),
        check_vma=False,
    )
```

```python
import math

import jax
import jax.numpy as jnp
import ml_dtypes
import numpy as np
from jax import lax
from jax.experimental import pallas as pl
from jax.experimental.pallas import tpu as pltpu
from jax.sharding import PartitionSpec as P

MESH = pl.DeviceIdType.MESH
DIAG, INWARD, SHARED = 0, 1, 2
FREQ = 384
LENGTH = 2 * FREQ


def tables(energies):
    freq = 2 * np.arange(FREQ)[:, None] + 1
    ahead = freq * np.arange(energies)[None, :] % (2 * LENGTH)
    back = (np.arange(energies) - energies // 2)[:, None] * freq.T % (2 * LENGTH)
    ahead = ahead * (math.pi / LENGTH)
    back = back * (math.pi / LENGTH)
    forward = np.concatenate([np.cos(ahead), np.sin(ahead)], axis=0)
    inverse = np.concatenate([np.cos(back), np.sin(back)], axis=1)
    return forward.astype(ml_dtypes.bfloat16), inverse.astype(ml_dtypes.bfloat16)


CHUNKS = ((DIAG, 0), (DIAG, 1), (SHARED, None), (INWARD, 0), (INWARD, 1))
D0, D1, S, I0, I1 = range(5)


def kernel(
    lesser,
    greater,
    coupling,
    forward_hbm,
    inverse_hbm,
    out,
    forward,
    inverse,
    graw,
    turned,
    xpass,
    ypass,
    xin,
    yin,
    pout,
    own,
    nearby,
    across,
    total,
    swap,
    wide,
    left,
    right,
    xcat,
    ycat,
    spec_one,
    spec_two,
    product,
    staged,
    sem_load,
    sem_keep,
    sem_raw,
    sem_pass,
    sem_x,
    sem_y,
    sem_p,
    sem_near,
    sem_across,
    sem_far,
    sem_out,
):
    row = lax.axis_index("row")
    col = lax.axis_index("col")
    en = lax.axis_index("en")
    me = col * 8 + en
    partner = row + 1 - 2 * lax.rem(row, 2)
    other = 3 - row
    far = lax.rem(row + 2, 4)
    inward = 1 - 2 * (row // 2)
    inner = lax.rem(lax.rem(row, 2) + row // 2, 2)
    is_inner = inner == 1
    is_outer = inner == 0
    slot_in, slot_out = 1 + inward, 1 - inward

    def peer(step):
        index = lax.rem(me + step, 32)
        return index, (row, index // 8, lax.rem(index, 8))

    def remote(src, dst, send, recv, target):
        return pltpu.make_async_remote_copy(
            src_ref=src,
            dst_ref=dst,
            send_sem=send,
            recv_sem=recv,
            device_id=target,
            device_id_type=MESH,
        )

    def across_rows(target):
        return (target, col, en)

    def bytes_of(ref, sem):
        pltpu.make_async_copy(ref, ref, sem).wait()

    load_diag = pltpu.make_async_copy(greater.at[:, 1], graw.at[DIAG], sem_load.at[0])
    load_forward = pltpu.make_async_copy(forward_hbm, forward, sem_load.at[1])
    load_inverse = pltpu.make_async_copy(inverse_hbm, inverse, sem_load.at[2])
    load_diag.start()

    @pl.when(is_outer)
    def _():
        pltpu.make_async_copy(greater.at[:, slot_in], graw.at[SHARED], sem_load.at[3]).start()

    @pl.when(is_inner)
    def _():
        pltpu.make_async_copy(lesser.at[:, slot_out, :, pl.ds(2, 2)], xpass, sem_load.at[4]).start()

    load_forward.start()
    load_inverse.start()

    barrier = pltpu.get_barrier_semaphore()

    def greet(step, carry):
        pl.semaphore_signal(barrier, inc=1, device_id=peer(step)[1], device_id_type=MESH)
        return carry

    lax.fori_loop(1, 32, greet, 0)
    for step in range(1, 4):
        pl.semaphore_signal(
            barrier, inc=1, device_id=across_rows(lax.rem(row + step, 4)), device_id_type=MESH
        )
    pl.semaphore_wait(barrier, 34)

    @pl.when(is_inner)
    def _():
        remote(
            lesser.at[:, slot_out, :, pl.ds(0, 2)], xpass, sem_pass.at[0], sem_pass.at[1], across_rows(partner)
        ).start()
        remote(
            greater.at[:, slot_out], graw.at[INWARD], sem_raw.at[0], sem_raw.at[2], across_rows(partner)
        ).start()
        remote(
            greater.at[:, slot_in], graw.at[INWARD], sem_raw.at[1], sem_raw.at[2], across_rows(other)
        ).start()

    def send_x(chunk):
        kind, half = CHUNKS[chunk]

        def source(to):
            if kind == SHARED:
                return xpass.at[:, to]
            return lesser.at[:, 1 if kind == DIAG else slot_in, to, pl.ds(2 * half, 2)]

        place = xin.at[chunk, :, :, pl.ds(64 * en, 64), :]

        def body(step, carry):
            to = lax.rem(en + step, 8)
            remote(source(to), place, sem_x.at[0, chunk], sem_x.at[1, chunk], (row, col, to)).start()
            return carry

        lax.fori_loop(1, 8, body, 0)
        pltpu.make_async_copy(source(en), place, sem_keep.at[0, chunk]).start()

    def send_y(chunk):
        kind, half = CHUNKS[chunk]

        def source(index):
            if kind == SHARED:
                return ypass.at[:, index]
            return turned.at[kind, :, index, pl.ds(32 * half, 32), :]

        def body(step, carry):
            index, target = peer(step)
            remote(
                source(index), yin.at[chunk, me], sem_y.at[0, chunk], sem_y.at[1, chunk], target
            ).start()
            return carry

        lax.fori_loop(1, 32, body, 0)
        pltpu.make_async_copy(source(me), yin.at[chunk, me], sem_keep.at[1, chunk]).start()

    def first_row(chunk):
        half = CHUNKS[chunk][1]
        return 2 * inner if half is None else 2 * half

    def parts_of(chunk):
        return ((0, 1), (1, 1)) if chunk == I1 else ((0, 2),)

    def send_p(chunk):
        kind = CHUNKS[chunk][0]
        for p, count in parts_of(chunk):
            place = own.at[kind, pl.ds(p, count), pl.ds(first_row(chunk), 2), me]

            def body(step, carry):
                index, target = peer(step)
                remote(
                    pout.at[chunk, pl.ds(p, count), :, pl.ds(16 * index, 16), :],
                    place,
                    sem_p.at[0, chunk, p],
                    sem_p.at[1, chunk, p],
                    target,
                ).start()
                return carry

            lax.fori_loop(1, 32, body, 0)
            pltpu.make_async_copy(
                pout.at[chunk, pl.ds(p, count), :, pl.ds(16 * me, 16), :], place, sem_keep.at[2 + p, chunk]
            ).start()

    def arrive(chunk):
        bytes_of(xin.at[chunk, :, :, pl.ds(0, 448), :], sem_x.at[1, chunk])
        bytes_of(xin.at[chunk, :, :, pl.ds(0, 64), :], sem_keep.at[0, chunk])
        bytes_of(yin.at[chunk, pl.ds(0, 31)], sem_y.at[1, chunk])
        bytes_of(yin.at[chunk, 0], sem_keep.at[1, chunk])

    def gather(chunk):
        kind = CHUNKS[chunk][0]
        for p, count in parts_of(chunk):
            bytes_of(own.at[kind, pl.ds(p, count), pl.ds(0, 2), pl.ds(0, 31)], sem_p.at[1, chunk, p])
            bytes_of(own.at[kind, pl.ds(p, count), pl.ds(0, 2), 0], sem_keep.at[2 + p, chunk])
            rows = pl.ds(first_row(chunk), 2)
            src = own.at[kind, pl.ds(p, count), rows]
            dst = src if kind == SHARED else nearby.at[kind, pl.ds(p, count), rows]
            remote(
                src, dst, sem_near.at[0, chunk, p], sem_near.at[1, chunk, p], across_rows(partner)
            ).start()

            @pl.when(is_inner)
            def _():
                remote(
                    src,
                    across.at[kind, pl.ds(p, count), rows],
                    sem_across.at[0, chunk, p],
                    sem_across.at[1, chunk, p],
                    across_rows(other),
                ).start()

            if chunk == S:

                @pl.when(is_outer)
                def _():
                    remote(
                        src, across.at[kind, :, pl.ds(0, 2)], sem_far.at[0], sem_far.at[1], across_rows(far)
                    ).start()

    def chunk_bytes(chunk, p, count):
        return own.at[CHUNKS[chunk][0], pl.ds(p, count), pl.ds(0, 2)]

    def from_partner(chunk, p):
        bytes_of(chunk_bytes(chunk, p, dict(parts_of(chunk))[p]), sem_near.at[1, chunk, p])

    def from_other(chunk, p):
        bytes_of(chunk_bytes(chunk, p, dict(parts_of(chunk))[p]), sem_across.at[1, chunk, p])

    def turn(kind):
        def part(p, carry):
            def one(s, inside):
                square = jnp.concatenate([graw[kind, p, s], graw[kind, p, s + 16]], axis=0).astype(jnp.float32)
                swap[pl.ds(s, 128, stride=16), :] = square.T
                return inside

            lax.fori_loop(0, 16, one, 0)
            turned[kind, p] = swap[...].astype(jnp.bfloat16).reshape(32, 64, 128)
            return carry

        lax.fori_loop(0, 2, part, 0)

    lane = lax.broadcasted_iota(jnp.int32, (16, 128), 1)

    def correlate(chunk):
        def body(a, carry):
            for p in range(2):
                xcat[:, p * 128 : (p + 1) * 128] = xin[chunk, p, a]
            for p in range(2):
                for c in range(4):
                    for k in range(4):
                        one = yin[chunk, c * 8 + 2 * k, p, pl.ds(16 * a, 16), :].astype(jnp.float32)
                        two = yin[chunk, c * 8 + 2 * k + 1, p, pl.ds(16 * a, 16), :].astype(jnp.float32)
                        first = jnp.where(lane < 64, one, pltpu.roll(two, 64, 1))
                        second = jnp.where(lane < 64, pltpu.roll(one, 64, 1), two)
                        base = p * 128 + c * 32
                        ycat[base : base + 16, k * 128 : (k + 1) * 128] = first.astype(jnp.bfloat16)
                        ycat[base + 16 : base + 32, k * 128 : (k + 1) * 128] = second.astype(jnp.bfloat16)
            spec_one[...] = jnp.dot(forward[...], xcat[...], preferred_element_type=jnp.float32)
            spec_two[...] = lax.dot_general(
                forward[...], ycat[...], (((1,), (1,)), ((), ())), preferred_element_type=jnp.float32
            )

            def mix(step, inner):
                cos_rows = pl.ds(step * 16, 16)
                sin_rows = pl.ds(FREQ + step * 16, 16)
                one_rr, one_ri = spec_one[cos_rows, 0:128], spec_one[cos_rows, 128:256]
                one_sr, one_si = spec_one[sin_rows, 0:128], spec_one[sin_rows, 128:256]
                two_rr, two_ri = spec_two[cos_rows, 0:128], spec_two[cos_rows, 128:256]
                two_sr, two_si = spec_two[sin_rows, 0:128], spec_two[sin_rows, 128:256]
                a_re, a_im = one_rr + one_si, one_ri - one_sr
                a_re_m, a_im_m = one_rr - one_si, one_ri + one_sr
                b_re, b_im = two_rr - two_si, two_ri + two_sr
                b_re_m, b_im_m = two_rr + two_si, two_ri - two_sr
                s_re = a_re * b_re - a_im * b_im
                s_im = a_re * b_im + a_im * b_re
                s_re_m = a_re_m * b_re_m - a_im_m * b_im_m
                s_im_m = a_re_m * b_im_m + a_im_m * b_re_m
                product[cos_rows, 0:128] = (s_re + s_re_m).astype(jnp.bfloat16)
                product[sin_rows, 0:128] = (s_im_m - s_im).astype(jnp.bfloat16)
                product[cos_rows, 128:256] = (s_im + s_im_m).astype(jnp.bfloat16)
                product[sin_rows, 128:256] = (s_re - s_re_m).astype(jnp.bfloat16)
                return inner

            lax.fori_loop(0, FREQ // 16, mix, 0)
            lagged = jnp.dot(inverse[...], product[...], preferred_element_type=jnp.float32)
            scale = 1.0 / (LENGTH * 32.0)
            pout[chunk, 0, a] = (scale * lagged[:, 128:256]).astype(jnp.bfloat16)
            pout[chunk, 1, a] = (-scale * lagged[:, 0:128]).astype(jnp.bfloat16)
            return carry

        lax.fori_loop(0, 2, body, 0)

    def apply_left(tile, side, column, parts=(0, 2)):
        def part(p, carry):
            swap[...] = tile[p].astype(jnp.float32).reshape(2048, 128)
            for pair in range(8):
                both = jnp.concatenate(
                    [
                        swap[pl.ds(2 * pair, 128, stride=16), :],
                        swap[pl.ds(2 * pair + 1, 128, stride=16), :],
                    ],
                    axis=1,
                ).astype(jnp.bfloat16)
                made = jnp.dot(left[side], both, preferred_element_type=jnp.float32)
                lower = pl.ds(256 * pair, 128)
                upper = pl.ds(256 * pair + 128, 128)
                total[p, column, lower, :] += made[:, 0:128]
                total[p, column, upper, :] += made[:, 128:256]
            return carry

        lax.fori_loop(*parts, part, 0)

    def finish(p):
        def block(quad, carry):
            rows = pl.ds(quad * 512, 512)
            whole = jnp.concatenate([total[p, b, rows, :].astype(jnp.bfloat16) for b in range(5)], axis=1)
            for s in range(5):
                low, high = max(s - 1, 0) * 128, min(s + 2, 5) * 128
                made = jnp.dot(
                    whole[:, low:high],
                    right[low:high, s * 128 : s * 128 + 128],
                    preferred_element_type=jnp.float32,
                )
                for lag in range(4):
                    wide[s, pl.ds(quad * 4 + lag, 128, stride=16), :] = made[lag * 128 : lag * 128 + 128]
            return carry

        lax.fori_loop(0, 4, block, 0)
        for s in range(5):
            staged[p, s] = wide[s].astype(jnp.bfloat16).reshape(128, 16, 128)
        pltpu.make_async_copy(staged.at[p], out.at[p, 0], sem_out.at[p]).start()

    send_x(D0)
    load_diag.wait()
    turn(DIAG)
    send_y(D0)
    send_x(D1)
    send_y(D1)

    @pl.when(is_outer)
    def _():
        bytes_of(graw.at[SHARED], sem_load.at[3])
        turn(SHARED)
        pltpu.make_async_copy(turned.at[SHARED, :, :, pl.ds(0, 32), :], ypass, sem_load.at[5]).start()
        remote(
            turned.at[SHARED, :, :, pl.ds(32, 32), :], ypass, sem_pass.at[2], sem_pass.at[3], across_rows(partner)
        ).start()

    place = lax.broadcasted_iota(jnp.int32, (128, 128), 1)
    orbital = lax.broadcasted_iota(jnp.int32, (128, 128), 0)
    order = (orbital == 4 * lax.rem(place, 32) + place // 32).astype(jnp.bfloat16)
    for side in range(3):
        left[side] = jnp.dot(coupling[row, side], order, preferred_element_type=jnp.float32).astype(jnp.bfloat16)
    for b in range(5):
        for s in range(max(b - 1, 0), min(b + 2, 5)):
            block = (slice(b * 128, b * 128 + 128), slice(s * 128, s * 128 + 128))
            tile_b, tile_c = row + b - 2, row + s - 2
            inside = ((tile_b >= 0) & (tile_b < 4) & (tile_c >= 0) & (tile_c < 4)).astype(jnp.float32)
            safe = jnp.clip(tile_c, 0, 3)
            tile = coupling[safe, b - s + 1].astype(jnp.float32) * inside
            right[block] = tile.T.astype(jnp.bfloat16)

    def clear(step, carry):
        for b in range(5):
            total[0, b, pl.ds(step * 256, 256), :] = jnp.zeros((256, 128), jnp.float32)
            total[1, b, pl.ds(step * 256, 256), :] = jnp.zeros((256, 128), jnp.float32)
        return carry

    lax.fori_loop(0, 8, clear, 0)
    load_forward.wait()
    load_inverse.wait()

    arrive(D0)
    correlate(D0)
    send_p(D0)

    @pl.when(is_outer)
    def _():
        bytes_of(xpass, sem_pass.at[1])
        bytes_of(ypass, sem_load.at[5])

    @pl.when(is_inner)
    def _():
        bytes_of(xpass, sem_load.at[4])
        bytes_of(ypass, sem_pass.at[3])

    send_x(S)
    send_y(S)
    bytes_of(graw.at[INWARD], sem_raw.at[2])
    turn(INWARD)
    arrive(D1)
    correlate(D1)
    send_p(D1)
    send_x(I0)
    send_y(I0)
    gather(D0)
    arrive(S)
    correlate(S)
    send_p(S)
    send_x(I1)
    send_y(I1)
    gather(D1)
    apply_left(own.at[DIAG], 1, 2)
    arrive(I0)
    correlate(I0)
    send_p(I0)
    gather(S)
    arrive(I1)
    correlate(I1)
    send_p(I1)
    gather(I0)

    toward = inward * (1 - 2 * inner)
    from_partner(D0, 0)
    from_partner(D1, 0)
    apply_left(nearby.at[DIAG], 1 + toward, 2 + toward)

    @pl.when(is_inner)
    def _():
        from_other(D0, 0)
        from_other(D1, 0)
        apply_left(across.at[DIAG], 1 + inward, 2 + inward)

    gather(I1)
    from_partner(S, 0)
    apply_left(own.at[SHARED], 1 + inward * (1 - inner), 2 - inward * inner)
    apply_left(own.at[INWARD], 1, 2 + inward)

    @pl.when(is_inner)
    def _():
        from_other(S, 0)
        bytes_of(chunk_bytes(S, 0, 2), sem_far.at[1])
        apply_left(across.at[SHARED], 1 + inward, 2 + 2 * inward)

    from_partner(I0, 0)

    @pl.when(is_inner)
    def _():
        from_other(I0, 0)

    for p in range(2):
        from_partner(I1, p)
        apply_left(nearby.at[INWARD], 1 + toward, 2 + 2 * inward * (1 - inner), (p, p + 1))

        @pl.when(is_inner)
        def _():
            from_other(I1, p)
            apply_left(across.at[INWARD], 1 + inward, 2, (p, p + 1))

        finish(p)

    for p in range(2):
        pltpu.make_async_copy(staged.at[p], out.at[p, 0], sem_out.at[p]).wait()

    @pl.when(is_inner)
    def _():
        bytes_of(xpass, sem_pass.at[0])
        bytes_of(graw.at[INWARD], sem_raw.at[0])
        bytes_of(graw.at[INWARD], sem_raw.at[1])

    @pl.when(is_outer)
    def _():
        bytes_of(ypass, sem_pass.at[2])
        bytes_of(chunk_bytes(S, 0, 2), sem_far.at[0])

    for chunk in range(5):
        kind = CHUNKS[chunk][0]
        bytes_of(xin.at[chunk, :, :, pl.ds(0, 448), :], sem_x.at[0, chunk])
        bytes_of(yin.at[chunk, pl.ds(0, 31)], sem_y.at[0, chunk])
        for p, count in parts_of(chunk):
            bytes_of(own.at[kind, pl.ds(p, count), pl.ds(0, 2), pl.ds(0, 31)], sem_p.at[0, chunk, p])
            bytes_of(chunk_bytes(chunk, p, count), sem_near.at[0, chunk, p])

            @pl.when(is_inner)
            def _():
                bytes_of(chunk_bytes(chunk, p, count), sem_across.at[0, chunk, p])


def shards(lesser, greater, coupling):
    forward, inverse = tables(512)
    half = jnp.bfloat16
    whole = jnp.float32
    anywhere = pl.BlockSpec(memory_space=pl.ANY)
    return pl.pallas_call(
        kernel,
        out_shape=jax.ShapeDtypeStruct((2, 1, 5, 128, 16, 128), half),
        in_specs=[anywhere, anywhere, pl.BlockSpec(memory_space=pltpu.VMEM), anywhere, anywhere],
        out_specs=anywhere,
        scratch_shapes=[
            pltpu.VMEM((LENGTH, 512), half),
            pltpu.VMEM((512, LENGTH), half),
            pltpu.VMEM((3, 2, 32, 64, 128), half),
            pltpu.VMEM((3, 2, 32, 64, 128), half),
            pltpu.VMEM((2, 8, 2, 64, 128), half),
            pltpu.VMEM((2, 32, 32, 128), half),
            pltpu.VMEM((5, 2, 2, 512, 128), half),
            pltpu.VMEM((5, 32, 2, 32, 128), half),
            pltpu.VMEM((5, 2, 2, 512, 128), half),
            pltpu.VMEM((3, 2, 4, 32, 16, 128), half),
            pltpu.VMEM((2, 2, 4, 32, 16, 128), half),
            pltpu.VMEM((3, 2, 4, 32, 16, 128), half),
            pltpu.VMEM((2, 5, 2048, 128), whole),
            pltpu.VMEM((2048, 128), whole),
            pltpu.VMEM((5, 2048, 128), whole),
            pltpu.VMEM((3, 128, 128), half),
            pltpu.VMEM((640, 640), half),
            pltpu.VMEM((512, 256), half),
            pltpu.VMEM((256, 512), half),
            pltpu.VMEM((LENGTH, 256), whole),
            pltpu.VMEM((LENGTH, 256), whole),
            pltpu.VMEM((LENGTH, 256), half),
            pltpu.VMEM((2, 5, 128, 16, 128), half),
            pltpu.SemaphoreType.DMA((6,)),
            pltpu.SemaphoreType.DMA((4, 5)),
            pltpu.SemaphoreType.DMA((3,)),
            pltpu.SemaphoreType.DMA((4,)),
            pltpu.SemaphoreType.DMA((2, 5)),
            pltpu.SemaphoreType.DMA((2, 5)),
            pltpu.SemaphoreType.DMA((2, 5, 2)),
            pltpu.SemaphoreType.DMA((2, 5, 2)),
            pltpu.SemaphoreType.DMA((2, 5, 2)),
            pltpu.SemaphoreType.DMA((2,)),
            pltpu.SemaphoreType.DMA((2,)),
        ],
        compiler_params=pltpu.CompilerParams(
            collective_id=0, has_side_effects=True, vmem_limit_bytes=60 * 1024 * 1024
        ),
        cost_estimate=pl.CostEstimate(flops=10**10, bytes_accessed=2 * 10**7, transcendentals=0),
    )(
        lesser.reshape(2, 3, 8, 4, 64, 128),
        greater.reshape(2, 3, 32, 64, 128),
        coupling,
        jnp.asarray(forward),
        jnp.asarray(inverse),
    )


def solution(mesh):
    placed = (P(None, "row", None, "col", "en", None), P(None, "row", None, "col", "en", None), P())
    return jax.shard_map(
        shards,
        mesh=mesh,
        in_specs=placed,
        out_specs=P(None, "row", None, None, ("col", "en"), None),
        check_vma=False,
    )
```

```python
import math

import jax
import jax.numpy as jnp
import ml_dtypes
import numpy as np
from jax import lax
from jax.experimental import pallas as pl
from jax.experimental.pallas import tpu as pltpu
from jax.sharding import PartitionSpec as P

MESH = pl.DeviceIdType.MESH
DIAG, INWARD, SHARED = 0, 1, 2
FREQ = 384
LENGTH = 2 * FREQ


def tables(energies):
    freq = 2 * np.arange(FREQ)[:, None] + 1
    ahead = freq * np.arange(energies)[None, :] % (2 * LENGTH)
    back = (np.arange(energies) - energies // 2)[:, None] * freq.T % (2 * LENGTH)
    ahead = ahead * (math.pi / LENGTH)
    back = back * (math.pi / LENGTH)
    forward = np.concatenate([np.cos(ahead), np.sin(ahead)], axis=0)
    inverse = np.concatenate([np.cos(back), np.sin(back)], axis=1)
    return forward.astype(ml_dtypes.bfloat16), inverse.astype(ml_dtypes.bfloat16)


CHUNKS = 10
AHEAD = 2


def kernel(
    lesser,
    greater,
    coupling,
    forward_hbm,
    inverse_hbm,
    out,
    forward,
    inverse,
    graw,
    turned,
    xpass,
    ypass,
    xin,
    yin,
    pout,
    own,
    nearby,
    across,
    total,
    swap,
    swap_two,
    mixed,
    wide,
    left,
    right,
    right_last,
    xcat,
    ycat,
    spec_one,
    spec_two,
    product,
    staged,
    sem_load,
    sem_keep,
    sem_raw,
    sem_pass,
    sem_x,
    sem_y,
    sem_p,
    sem_near,
    sem_across,
    sem_far,
    sem_out,
):
    row = lax.axis_index("row")
    col = lax.axis_index("col")
    en = lax.axis_index("en")
    me = col * 8 + en
    partner = row + 1 - 2 * lax.rem(row, 2)
    other = 3 - row
    far = lax.rem(row + 2, 4)
    inward = 1 - 2 * (row // 2)
    inner = lax.rem(lax.rem(row, 2) + row // 2, 2)
    is_inner = inner == 1
    is_outer = inner == 0
    slot_in, slot_out = 1 + inward, 1 - inward
    toward = inward * (1 - 2 * inner)
    last = 2 + 2 * inward * (1 - inner)

    def peer(step):
        index = lax.rem(me + step, 32)
        return index, (row, index // 8, lax.rem(index, 8))

    def remote(src, dst, send, recv, target):
        return pltpu.make_async_remote_copy(
            src_ref=src,
            dst_ref=dst,
            send_sem=send,
            recv_sem=recv,
            device_id=target,
            device_id_type=MESH,
        )

    def across_rows(target):
        return (target, col, en)

    def bytes_of(ref, sem):
        pltpu.make_async_copy(ref, ref, sem).wait()

    load_diag = pltpu.make_async_copy(greater.at[:, 1], graw.at[DIAG], sem_load.at[0])
    load_forward = pltpu.make_async_copy(forward_hbm, forward, sem_load.at[1])
    load_inverse = pltpu.make_async_copy(inverse_hbm, inverse, sem_load.at[2])
    load_diag.start()

    @pl.when(is_outer)
    def _():
        pltpu.make_async_copy(greater.at[:, slot_in], graw.at[SHARED], sem_load.at[3]).start()

    @pl.when(is_inner)
    def _():
        pltpu.make_async_copy(lesser.at[:, slot_out, :, pl.ds(2, 2)], xpass, sem_load.at[4]).start()

    load_forward.start()
    load_inverse.start()

    barrier = pltpu.get_barrier_semaphore()

    def greet(step, carry):
        pl.semaphore_signal(barrier, inc=1, device_id=peer(step)[1], device_id_type=MESH)
        return carry

    lax.fori_loop(1, 32, greet, 0)
    for step in range(1, 4):
        pl.semaphore_signal(
            barrier, inc=1, device_id=across_rows(lax.rem(row + step, 4)), device_id_type=MESH
        )
    pl.semaphore_wait(barrier, 34)

    @pl.when(is_inner)
    def _():
        remote(
            lesser.at[:, slot_out, :, pl.ds(0, 2)], xpass, sem_pass.at[0], sem_pass.at[1], across_rows(partner)
        ).start()
        remote(
            greater.at[:, slot_out], graw.at[INWARD], sem_raw.at[0], sem_raw.at[2], across_rows(partner)
        ).start()
        remote(
            greater.at[:, slot_in], graw.at[INWARD], sem_raw.at[1], sem_raw.at[2], across_rows(other)
        ).start()

    def is_kind(chunk, kind):
        if kind == DIAG:
            return chunk < 4
        if kind == SHARED:
            return (chunk >= 4) & (chunk < 6)
        return chunk >= 6

    def place_of(chunk):
        shared = (chunk >= 4).astype(jnp.int32) - (chunk >= 6).astype(jnp.int32)
        return chunk + 2 * inner * shared + 2 * (chunk >= 6).astype(jnp.int32)

    def send_x(chunk):
        place = xin.at[chunk, :, pl.ds(64 * en, 64), :]

        def spread(source):
            def body(step, carry):
                to = lax.rem(en + step, 8)
                remote(source(to), place, sem_x.at[0, chunk], sem_x.at[1, chunk], (row, col, to)).start()
                return carry

            lax.fori_loop(1, 8, body, 0)
            pltpu.make_async_copy(source(en), place, sem_keep.at[0, chunk]).start()

        @pl.when(is_kind(chunk, SHARED))
        def _():
            spread(lambda to: xpass.at[:, to, chunk - 4])

        @pl.when(jnp.logical_not(is_kind(chunk, SHARED)))
        def _():
            inside = (chunk >= 6).astype(jnp.int32)
            spread(lambda to: lesser.at[:, 1 + inside * inward, to, chunk - 6 * inside])

    def send_y(chunk):
        place = yin.at[chunk, me]

        def spread(source):
            def body(step, carry):
                index, target = peer(step)
                remote(source(index), place, sem_y.at[0, chunk], sem_y.at[1, chunk], target).start()
                return carry

            lax.fori_loop(1, 32, body, 0)
            pltpu.make_async_copy(source(me), place, sem_keep.at[1, chunk]).start()

        @pl.when(is_kind(chunk, SHARED))
        def _():
            spread(lambda index: ypass.at[:, index, pl.ds(16 * (chunk - 4), 16), :])

        @pl.when(jnp.logical_not(is_kind(chunk, SHARED)))
        def _():
            inside = (chunk >= 6).astype(jnp.int32)
            spread(lambda index: turned.at[inside, :, index, pl.ds(16 * (chunk - 6 * inside), 16), :])

    def send_p(chunk):
        place = own.at[place_of(chunk), :, me]

        def body(step, carry):
            index, target = peer(step)
            remote(
                pout.at[chunk, :, pl.ds(16 * index, 16), :], place, sem_p.at[0, chunk], sem_p.at[1, chunk], target
            ).start()
            return carry

        lax.fori_loop(1, 32, body, 0)
        pltpu.make_async_copy(pout.at[chunk, :, pl.ds(16 * me, 16), :], place, sem_keep.at[2, chunk]).start()

    def arrive(chunk):
        bytes_of(xin.at[chunk, :, pl.ds(0, 448), :], sem_x.at[1, chunk])
        bytes_of(xin.at[chunk, :, pl.ds(0, 64), :], sem_keep.at[0, chunk])
        bytes_of(yin.at[chunk, pl.ds(0, 31)], sem_y.at[1, chunk])
        bytes_of(yin.at[chunk, 0], sem_keep.at[1, chunk])

    def gather(chunk):
        bytes_of(own.at[0, :, pl.ds(0, 31)], sem_p.at[1, chunk])
        bytes_of(own.at[0, :, 0], sem_keep.at[2, chunk])
        place = place_of(chunk)
        src = own.at[place]

        def to_partner(dst):
            remote(
                src, dst.at[place], sem_near.at[0, chunk], sem_near.at[1, chunk], across_rows(partner)
            ).start()

        @pl.when(is_kind(chunk, SHARED))
        def _():
            to_partner(own)

        @pl.when(jnp.logical_not(is_kind(chunk, SHARED)))
        def _():
            to_partner(nearby)

        @pl.when(is_inner)
        def _():
            remote(
                src, across.at[place], sem_across.at[0, chunk], sem_across.at[1, chunk], across_rows(other)
            ).start()

        @pl.when(is_outer & is_kind(chunk, SHARED))
        def _():
            remote(
                src, across.at[place], sem_far.at[0, chunk - 4], sem_far.at[1, chunk - 4], across_rows(far)
            ).start()

    def from_partner(chunk):
        bytes_of(own.at[0], sem_near.at[1, chunk])

    def from_other(chunk):
        bytes_of(own.at[0], sem_across.at[1, chunk])

    def turn(kind):
        def part(p, carry):
            def one(s, inside):
                square = jnp.concatenate([graw[kind, p, s], graw[kind, p, s + 16]], axis=0).astype(jnp.float32)
                swap[pl.ds(s, 128, stride=16), :] = square.T
                return inside

            lax.fori_loop(0, 16, one, 0)
            turned[kind, p] = swap[...].astype(jnp.bfloat16).reshape(32, 64, 128)
            return carry

        lax.fori_loop(0, 2, part, 0)

    lane = lax.broadcasted_iota(jnp.int32, (16, 128), 1)

    def correlate(chunk):
        for p in range(2):
            xcat[:, p * 128 : (p + 1) * 128] = xin[chunk, p]
        for p in range(2):
            for c in range(4):
                for k in range(4):
                    one = yin[chunk, c * 8 + 2 * k, p].astype(jnp.float32)
                    two = yin[chunk, c * 8 + 2 * k + 1, p].astype(jnp.float32)
                    first = jnp.where(lane < 64, one, pltpu.roll(two, 64, 1))
                    second = jnp.where(lane < 64, pltpu.roll(one, 64, 1), two)
                    base = p * 128 + c * 32
                    ycat[base : base + 16, k * 128 : (k + 1) * 128] = first.astype(jnp.bfloat16)
                    ycat[base + 16 : base + 32, k * 128 : (k + 1) * 128] = second.astype(jnp.bfloat16)
        spec_one[...] = jnp.dot(forward[...], xcat[...], preferred_element_type=jnp.float32)
        spec_two[...] = lax.dot_general(
            forward[...], ycat[...], (((1,), (1,)), ((), ())), preferred_element_type=jnp.float32
        )

        def mix(step, inner):
            cos_rows = pl.ds(step * 16, 16)
            sin_rows = pl.ds(FREQ + step * 16, 16)
            one_rr, one_ri = spec_one[cos_rows, 0:128], spec_one[cos_rows, 128:256]
            one_sr, one_si = spec_one[sin_rows, 0:128], spec_one[sin_rows, 128:256]
            two_rr, two_ri = spec_two[cos_rows, 0:128], spec_two[cos_rows, 128:256]
            two_sr, two_si = spec_two[sin_rows, 0:128], spec_two[sin_rows, 128:256]
            a_re, a_im = one_rr + one_si, one_ri - one_sr
            a_re_m, a_im_m = one_rr - one_si, one_ri + one_sr
            b_re, b_im = two_rr - two_si, two_ri + two_sr
            b_re_m, b_im_m = two_rr + two_si, two_ri - two_sr
            s_re = a_re * b_re - a_im * b_im
            s_im = a_re * b_im + a_im * b_re
            s_re_m = a_re_m * b_re_m - a_im_m * b_im_m
            s_im_m = a_re_m * b_im_m + a_im_m * b_re_m
            product[cos_rows, 0:128] = (s_re + s_re_m).astype(jnp.bfloat16)
            product[sin_rows, 0:128] = (s_im_m - s_im).astype(jnp.bfloat16)
            product[cos_rows, 128:256] = (s_im + s_im_m).astype(jnp.bfloat16)
            product[sin_rows, 128:256] = (s_re - s_re_m).astype(jnp.bfloat16)
            return inner

        lax.fori_loop(0, FREQ // 16, mix, 0)
        lagged = jnp.dot(inverse[...], product[...], preferred_element_type=jnp.float32)
        scale = 1.0 / (LENGTH * 32.0)
        pout[chunk, 0] = (scale * lagged[:, 128:256]).astype(jnp.bfloat16)
        pout[chunk, 1] = (-scale * lagged[:, 0:128]).astype(jnp.bfloat16)

    def apply_left(tiles, kind, side, column, parts=(0, 2)):
        def part(p, carry):
            swap[...] = tiles[pl.ds(4 * kind, 4), p].astype(jnp.float32).reshape(2048, 128)
            for pair in range(8):
                both = jnp.concatenate(
                    [
                        swap[pl.ds(2 * pair, 128, stride=16), :],
                        swap[pl.ds(2 * pair + 1, 128, stride=16), :],
                    ],
                    axis=1,
                ).astype(jnp.bfloat16)
                made = jnp.dot(left[side], both, preferred_element_type=jnp.float32)
                lower = pl.ds(256 * pair, 128)
                upper = pl.ds(256 * pair + 128, 128)
                total[p, column, lower, :] += made[:, 0:128]
                total[p, column, upper, :] += made[:, 128:256]
            return carry

        lax.fori_loop(*parts, part, 0)

    def finish_early(p, carry):
        def block(quad, inside):
            rows = pl.ds(quad * 512, 512)
            whole = jnp.concatenate([total[p, b, rows, :].astype(jnp.bfloat16) for b in range(5)], axis=1)
            for s in range(5):
                low, high = max(s - 1, 0) * 128, min(s + 2, 5) * 128
                made = jnp.dot(
                    whole[:, low:high],
                    right[low:high, s * 128 : s * 128 + 128],
                    preferred_element_type=jnp.float32,
                )
                for lag in range(4):
                    wide[p, s, pl.ds(quad * 4 + lag, 128, stride=16), :] = made[lag * 128 : lag * 128 + 128]
            return inside

        lax.fori_loop(0, 4, block, 0)
        for s in range(5):

            @pl.when((s < last - 1) | (s > last + 1))
            def _():
                staged[p, s] = wide[p, s].astype(jnp.bfloat16).reshape(128, 16, 128)
                pltpu.make_async_copy(staged.at[p, s], out.at[p, 0, s], sem_out.at[p, s]).start()

        return carry

    def finish_last(p, carry):
        swap[...] = nearby[pl.ds(8, 4), p].astype(jnp.float32).reshape(2048, 128)
        swap_two[...] = across[pl.ds(8, 4), p].astype(jnp.float32).reshape(2048, 128)
        both_left = jnp.concatenate([left[1 + toward], left[1 + inward]], axis=1)
        for pair in range(8):
            both = jnp.concatenate(
                [
                    jnp.concatenate(
                        [
                            held[pl.ds(2 * pair, 128, stride=16), :],
                            held[pl.ds(2 * pair + 1, 128, stride=16), :],
                        ],
                        axis=1,
                    )
                    for held in (swap, swap_two)
                ],
                axis=0,
            ).astype(jnp.bfloat16)
            made = jnp.dot(both_left, both, preferred_element_type=jnp.float32)
            lower = pl.ds(256 * pair, 128)
            upper = pl.ds(256 * pair + 128, 128)
            mixed[pl.ds(2 * pair, 128, stride=16), :] = made[:, 0:128] + total[p, last, lower, :]
            mixed[pl.ds(2 * pair + 1, 128, stride=16), :] = made[:, 128:256] + total[p, last, upper, :]
        for near in range(3):
            s = last + near - 1

            @pl.when((s >= 0) & (s < 5))
            def _():
                made = jnp.dot(
                    mixed[...].astype(jnp.bfloat16), right_last[near], preferred_element_type=jnp.float32
                )
                staged[p, s] = (wide[p, s] + made).astype(jnp.bfloat16).reshape(128, 16, 128)
                pltpu.make_async_copy(staged.at[p, s], out.at[p, 0, s], sem_out.at[p, s]).start()

        return carry

    send_x(jnp.int32(0))
    send_x(jnp.int32(1))
    load_diag.wait()
    turn(DIAG)
    send_y(jnp.int32(0))
    send_y(jnp.int32(1))

    @pl.when(is_outer)
    def _():
        bytes_of(graw.at[SHARED], sem_load.at[3])
        turn(SHARED)
        pltpu.make_async_copy(turned.at[SHARED, :, :, pl.ds(0, 32), :], ypass, sem_load.at[5]).start()
        remote(
            turned.at[SHARED, :, :, pl.ds(32, 32), :], ypass, sem_pass.at[2], sem_pass.at[3], across_rows(partner)
        ).start()

    place = lax.broadcasted_iota(jnp.int32, (128, 128), 1)
    orbital = lax.broadcasted_iota(jnp.int32, (128, 128), 0)
    order = (orbital == 4 * lax.rem(place, 32) + place // 32).astype(jnp.bfloat16)
    for side in range(3):
        left[side] = jnp.dot(coupling[row, side], order, preferred_element_type=jnp.float32).astype(jnp.bfloat16)
    for b in range(5):
        for s in range(max(b - 1, 0), min(b + 2, 5)):
            block = (slice(b * 128, b * 128 + 128), slice(s * 128, s * 128 + 128))
            tile_b, tile_c = row + b - 2, row + s - 2
            inside = (
                (tile_b >= 0) & (tile_b < 4) & (tile_c >= 0) & (tile_c < 4) & (b != last)
            ).astype(jnp.float32)
            safe = jnp.clip(tile_c, 0, 3)
            tile = coupling[safe, b - s + 1].astype(jnp.float32) * inside
            right[block] = tile.T.astype(jnp.bfloat16)

    for near in range(3):
        tile_b, tile_c = row + last - 2, row + last - 2 + near - 1
        inside = ((tile_c >= 0) & (tile_c < 4)).astype(jnp.float32)
        tile = coupling[jnp.clip(tile_c, 0, 3), 2 - near].astype(jnp.float32) * inside
        right_last[near] = tile.T.astype(jnp.bfloat16)

    @pl.when(is_outer)
    def _():
        for place in range(8, 12):
            across[place] = jnp.zeros((2, 32, 16, 128), jnp.bfloat16)

    def clear(step, carry):
        for b in range(5):
            total[0, b, pl.ds(step * 256, 256), :] = jnp.zeros((256, 128), jnp.float32)
            total[1, b, pl.ds(step * 256, 256), :] = jnp.zeros((256, 128), jnp.float32)
        return carry

    lax.fori_loop(0, 8, clear, 0)
    load_forward.wait()
    load_inverse.wait()


    def step(chunk, carry):
        arrive(chunk)
        correlate(chunk)
        send_p(chunk)
        ahead = chunk + AHEAD

        @pl.when(ahead == 4)
        def _():
            @pl.when(is_outer)
            def _():
                bytes_of(xpass, sem_pass.at[1])
                bytes_of(ypass, sem_load.at[5])

            @pl.when(is_inner)
            def _():
                bytes_of(xpass, sem_load.at[4])
                bytes_of(ypass, sem_pass.at[3])

        @pl.when(ahead == 6)
        def _():
            bytes_of(graw.at[INWARD], sem_raw.at[2])
            turn(INWARD)

        @pl.when(ahead < CHUNKS)
        def _():
            send_x(ahead)
            send_y(ahead)

        @pl.when(chunk >= 1)
        def _():
            gather(chunk - 1)

        @pl.when(chunk == 6)
        def _():
            apply_left(own, 0, 1, 2)

        @pl.when(chunk == 9)
        def _():
            for early in range(4):
                from_partner(early)
            apply_left(nearby, 0, 1 + toward, 2 + toward)

        return carry

    lax.fori_loop(0, CHUNKS, step, 0)

    @pl.when(is_inner)
    def _():
        for early in range(4):
            from_other(early)
        apply_left(across, 0, 1 + inward, 2 + inward)

    gather(jnp.int32(9))
    from_partner(4)
    from_partner(5)
    apply_left(own, 1, 1 + inward * (1 - inner), 2 - inward * inner)
    apply_left(own, 2, 1, 2 + inward)

    @pl.when(is_inner)
    def _():
        for chunk in range(4, 6):
            from_other(chunk)
            bytes_of(own.at[0], sem_far.at[1, chunk - 4])
        apply_left(across, 1, 1 + inward, 2 + 2 * inward)

    lax.fori_loop(0, 2, finish_early, 0)
    for chunk in range(6, CHUNKS):
        from_partner(chunk)

    @pl.when(is_inner)
    def _():
        for chunk in range(6, CHUNKS):
            from_other(chunk)

    lax.fori_loop(0, 2, finish_last, 0)
    for p in range(2):
        for s in range(5):
            pltpu.make_async_copy(staged.at[p, s], out.at[p, 0, s], sem_out.at[p, s]).wait()

    @pl.when(is_inner)
    def _():
        bytes_of(xpass, sem_pass.at[0])
        bytes_of(graw.at[INWARD], sem_raw.at[0])
        bytes_of(graw.at[INWARD], sem_raw.at[1])

    @pl.when(is_outer)
    def _():
        bytes_of(ypass, sem_pass.at[2])
        for chunk in range(4, 6):
            bytes_of(own.at[0], sem_far.at[0, chunk - 4])

    def sent(chunk, carry):
        bytes_of(xin.at[chunk, :, pl.ds(0, 448), :], sem_x.at[0, chunk])
        bytes_of(yin.at[chunk, pl.ds(0, 31)], sem_y.at[0, chunk])
        bytes_of(own.at[0, :, pl.ds(0, 31)], sem_p.at[0, chunk])
        bytes_of(own.at[0], sem_near.at[0, chunk])

        @pl.when(is_inner)
        def _():
            bytes_of(own.at[0], sem_across.at[0, chunk])

        return carry

    lax.fori_loop(0, CHUNKS, sent, 0)


def shards(lesser, greater, coupling):
    forward, inverse = tables(512)
    half = jnp.bfloat16
    whole = jnp.float32
    anywhere = pl.BlockSpec(memory_space=pl.ANY)
    return pl.pallas_call(
        kernel,
        out_shape=jax.ShapeDtypeStruct((2, 1, 5, 128, 16, 128), half),
        in_specs=[anywhere, anywhere, pl.BlockSpec(memory_space=pltpu.VMEM), anywhere, anywhere],
        out_specs=anywhere,
        scratch_shapes=[
            pltpu.VMEM((LENGTH, 512), half),
            pltpu.VMEM((512, LENGTH), half),
            pltpu.VMEM((3, 2, 32, 64, 128), half),
            pltpu.VMEM((3, 2, 32, 64, 128), half),
            pltpu.VMEM((2, 8, 2, 64, 128), half),
            pltpu.VMEM((2, 32, 32, 128), half),
            pltpu.VMEM((CHUNKS, 2, 512, 128), half),
            pltpu.VMEM((CHUNKS, 32, 2, 16, 128), half),
            pltpu.VMEM((CHUNKS, 2, 512, 128), half),
            pltpu.VMEM((12, 2, 32, 16, 128), half),
            pltpu.VMEM((12, 2, 32, 16, 128), half),
            pltpu.VMEM((12, 2, 32, 16, 128), half),
            pltpu.VMEM((2, 5, 2048, 128), whole),
            pltpu.VMEM((2048, 128), whole),
            pltpu.VMEM((2048, 128), whole),
            pltpu.VMEM((2048, 128), whole),
            pltpu.VMEM((2, 5, 2048, 128), whole),
            pltpu.VMEM((3, 128, 128), half),
            pltpu.VMEM((640, 640), half),
            pltpu.VMEM((3, 128, 128), half),
            pltpu.VMEM((512, 256), half),
            pltpu.VMEM((256, 512), half),
            pltpu.VMEM((LENGTH, 256), whole),
            pltpu.VMEM((LENGTH, 256), whole),
            pltpu.VMEM((LENGTH, 256), half),
            pltpu.VMEM((2, 5, 128, 16, 128), half),
            pltpu.SemaphoreType.DMA((6,)),
            pltpu.SemaphoreType.DMA((3, CHUNKS)),
            pltpu.SemaphoreType.DMA((3,)),
            pltpu.SemaphoreType.DMA((4,)),
            pltpu.SemaphoreType.DMA((2, CHUNKS)),
            pltpu.SemaphoreType.DMA((2, CHUNKS)),
            pltpu.SemaphoreType.DMA((2, CHUNKS)),
            pltpu.SemaphoreType.DMA((2, CHUNKS)),
            pltpu.SemaphoreType.DMA((2, CHUNKS)),
            pltpu.SemaphoreType.DMA((2, 2)),
            pltpu.SemaphoreType.DMA((2, 5)),
        ],
        compiler_params=pltpu.CompilerParams(
            collective_id=0, has_side_effects=True, vmem_limit_bytes=60 * 1024 * 1024
        ),
        cost_estimate=pl.CostEstimate(flops=10**10, bytes_accessed=2 * 10**7, transcendentals=0),
    )(
        lesser.reshape(2, 3, 8, 4, 64, 128),
        greater.reshape(2, 3, 32, 64, 128),
        coupling,
        jnp.asarray(forward),
        jnp.asarray(inverse),
    )


def solution(mesh):
    placed = (P(None, "row", None, "col", "en", None), P(None, "row", None, "col", "en", None), P())
    return jax.shard_map(
        shards,
        mesh=mesh,
        in_specs=placed,
        out_specs=P(None, "row", None, None, ("col", "en"), None),
        check_vma=False,
    )
```

```python
import math

import jax
import jax.numpy as jnp
import ml_dtypes
import numpy as np
from jax import lax
from jax.experimental import pallas as pl
from jax.experimental.pallas import tpu as pltpu
from jax.sharding import PartitionSpec as P

MESH = pl.DeviceIdType.MESH
DIAG, INWARD, SHARED = 0, 1, 2
FREQ = 384
LENGTH = 2 * FREQ


def tables(energies):
    freq = 2 * np.arange(FREQ)[:, None] + 1
    ahead = freq * np.arange(energies)[None, :] % (2 * LENGTH)
    back = (np.arange(energies) - energies // 2)[:, None] * freq.T % (2 * LENGTH)
    ahead = ahead * (math.pi / LENGTH)
    back = back * (math.pi / LENGTH)
    forward = np.concatenate([np.cos(ahead), np.sin(ahead)], axis=0)
    inverse = np.concatenate([np.cos(back), np.sin(back)], axis=1)
    return forward.astype(ml_dtypes.bfloat16), inverse.astype(ml_dtypes.bfloat16)


CHUNKS = 10
AHEAD = 2


def kernel(
    lesser,
    greater,
    coupling,
    forward_hbm,
    inverse_hbm,
    out,
    forward,
    inverse,
    graw,
    turned,
    xpass,
    ypass,
    xin,
    yin,
    pout,
    own,
    nearby,
    across,
    total,
    swap,
    swap_two,
    mixed,
    wide,
    left,
    right,
    right_last,
    xcat,
    ycat,
    spec_one,
    spec_two,
    product,
    sem_load,
    sem_keep,
    sem_raw,
    sem_pass,
    sem_x,
    sem_y,
    sem_p,
    sem_near,
    sem_across,
    sem_far,
):
    row = lax.axis_index("row")
    col = lax.axis_index("col")
    en = lax.axis_index("en")
    me = col * 8 + en
    partner = row + 1 - 2 * lax.rem(row, 2)
    other = 3 - row
    far = lax.rem(row + 2, 4)
    inward = 1 - 2 * (row // 2)
    inner = lax.rem(lax.rem(row, 2) + row // 2, 2)
    is_inner = inner == 1
    is_outer = inner == 0
    slot_in, slot_out = 1 + inward, 1 - inward
    toward = inward * (1 - 2 * inner)
    last = 2 + 2 * inward * (1 - inner)

    def peer(step):
        index = lax.rem(me + step, 32)
        return index, (row, index // 8, lax.rem(index, 8))

    def remote(src, dst, send, recv, target):
        return pltpu.make_async_remote_copy(
            src_ref=src,
            dst_ref=dst,
            send_sem=send,
            recv_sem=recv,
            device_id=target,
            device_id_type=MESH,
        )

    def across_rows(target):
        return (target, col, en)

    def bytes_of(ref, sem):
        pltpu.make_async_copy(ref, ref, sem).wait()

    load_diag = pltpu.make_async_copy(greater.at[:, 1], graw.at[DIAG], sem_load.at[0])
    load_forward = pltpu.make_async_copy(forward_hbm, forward, sem_load.at[1])
    load_inverse = pltpu.make_async_copy(inverse_hbm, inverse, sem_load.at[2])
    load_diag.start()

    @pl.when(is_outer)
    def _():
        pltpu.make_async_copy(greater.at[:, slot_in], graw.at[SHARED], sem_load.at[3]).start()

    @pl.when(is_inner)
    def _():
        pltpu.make_async_copy(lesser.at[:, slot_out, :, pl.ds(2, 2)], xpass, sem_load.at[4]).start()

    load_forward.start()
    load_inverse.start()

    barrier = pltpu.get_barrier_semaphore()

    def greet(step, carry):
        pl.semaphore_signal(barrier, inc=1, device_id=peer(step)[1], device_id_type=MESH)
        return carry

    lax.fori_loop(1, 32, greet, 0)
    for step in range(1, 4):
        pl.semaphore_signal(
            barrier, inc=1, device_id=across_rows(lax.rem(row + step, 4)), device_id_type=MESH
        )
    pl.semaphore_wait(barrier, 34)

    @pl.when(is_inner)
    def _():
        remote(
            lesser.at[:, slot_out, :, pl.ds(0, 2)], xpass, sem_pass.at[0], sem_pass.at[1], across_rows(partner)
        ).start()
        remote(
            greater.at[:, slot_out], graw.at[INWARD], sem_raw.at[0], sem_raw.at[2], across_rows(partner)
        ).start()
        remote(
            greater.at[:, slot_in], graw.at[INWARD], sem_raw.at[1], sem_raw.at[2], across_rows(other)
        ).start()

    def is_kind(chunk, kind):
        if kind == DIAG:
            return chunk < 4
        if kind == SHARED:
            return (chunk >= 4) & (chunk < 6)
        return chunk >= 6

    def place_of(chunk):
        shared = (chunk >= 4).astype(jnp.int32) - (chunk >= 6).astype(jnp.int32)
        return chunk + 2 * inner * shared + 2 * (chunk >= 6).astype(jnp.int32)

    def send_x(chunk):
        place = xin.at[chunk, :, pl.ds(64 * en, 64), :]

        def spread(source):
            def body(step, carry):
                to = lax.rem(en + step, 8)
                remote(source(to), place, sem_x.at[0, chunk], sem_x.at[1, chunk], (row, col, to)).start()
                return carry

            lax.fori_loop(1, 8, body, 0)
            pltpu.make_async_copy(source(en), place, sem_keep.at[0, chunk]).start()

        @pl.when(is_kind(chunk, SHARED))
        def _():
            spread(lambda to: xpass.at[:, to, chunk - 4])

        @pl.when(jnp.logical_not(is_kind(chunk, SHARED)))
        def _():
            inside = (chunk >= 6).astype(jnp.int32)
            spread(lambda to: lesser.at[:, 1 + inside * inward, to, chunk - 6 * inside])

    def send_y(chunk):
        place = yin.at[chunk, me]

        def spread(source):
            def body(step, carry):
                index, target = peer(step)
                remote(source(index), place, sem_y.at[0, chunk], sem_y.at[1, chunk], target).start()
                return carry

            lax.fori_loop(1, 32, body, 0)
            pltpu.make_async_copy(source(me), place, sem_keep.at[1, chunk]).start()

        @pl.when(is_kind(chunk, SHARED))
        def _():
            spread(lambda index: ypass.at[:, index, pl.ds(16 * (chunk - 4), 16), :])

        @pl.when(jnp.logical_not(is_kind(chunk, SHARED)))
        def _():
            inside = (chunk >= 6).astype(jnp.int32)
            spread(lambda index: turned.at[inside, :, index, pl.ds(16 * (chunk - 6 * inside), 16), :])

    def send_p(chunk):
        place = own.at[place_of(chunk), :, me]

        def body(step, carry):
            index, target = peer(step)
            remote(
                pout.at[chunk, :, pl.ds(16 * index, 16), :], place, sem_p.at[0, chunk], sem_p.at[1, chunk], target
            ).start()
            return carry

        lax.fori_loop(1, 32, body, 0)
        pltpu.make_async_copy(pout.at[chunk, :, pl.ds(16 * me, 16), :], place, sem_keep.at[2, chunk]).start()

    def arrive(chunk):
        bytes_of(xin.at[chunk, :, pl.ds(0, 448), :], sem_x.at[1, chunk])
        bytes_of(xin.at[chunk, :, pl.ds(0, 64), :], sem_keep.at[0, chunk])
        bytes_of(yin.at[chunk, pl.ds(0, 31)], sem_y.at[1, chunk])
        bytes_of(yin.at[chunk, 0], sem_keep.at[1, chunk])

    def gather(chunk):
        bytes_of(own.at[0, :, pl.ds(0, 31)], sem_p.at[1, chunk])
        bytes_of(own.at[0, :, 0], sem_keep.at[2, chunk])
        place = place_of(chunk)
        src = own.at[place]

        def to_partner(dst):
            remote(
                src, dst.at[place], sem_near.at[0, chunk], sem_near.at[1, chunk], across_rows(partner)
            ).start()

        @pl.when(is_kind(chunk, SHARED))
        def _():
            to_partner(own)

        @pl.when(jnp.logical_not(is_kind(chunk, SHARED)))
        def _():
            to_partner(nearby)

        @pl.when(is_inner)
        def _():
            remote(
                src, across.at[place], sem_across.at[0, chunk], sem_across.at[1, chunk], across_rows(other)
            ).start()

        @pl.when(is_outer & is_kind(chunk, SHARED))
        def _():
            remote(
                src, across.at[place], sem_far.at[0, chunk - 4], sem_far.at[1, chunk - 4], across_rows(far)
            ).start()

    def from_partner(chunk):
        bytes_of(own.at[0], sem_near.at[1, chunk])

    def from_other(chunk):
        bytes_of(own.at[0], sem_across.at[1, chunk])

    def turn(kind):
        def part(p, carry):
            def one(s, inside):
                square = jnp.concatenate([graw[kind, p, s], graw[kind, p, s + 16]], axis=0).astype(jnp.float32)
                swap[pl.ds(s, 128, stride=16), :] = square.T
                return inside

            lax.fori_loop(0, 16, one, 0)
            turned[kind, p] = swap[...].astype(jnp.bfloat16).reshape(32, 64, 128)
            return carry

        lax.fori_loop(0, 2, part, 0)

    lane = lax.broadcasted_iota(jnp.int32, (16, 128), 1)

    def correlate(chunk):
        for p in range(2):
            xcat[:, p * 128 : (p + 1) * 128] = xin[chunk, p]
        for p in range(2):
            for c in range(4):
                for k in range(4):
                    one = yin[chunk, c * 8 + 2 * k, p].astype(jnp.float32)
                    two = yin[chunk, c * 8 + 2 * k + 1, p].astype(jnp.float32)
                    first = jnp.where(lane < 64, one, pltpu.roll(two, 64, 1))
                    second = jnp.where(lane < 64, pltpu.roll(one, 64, 1), two)
                    base = p * 128 + c * 32
                    ycat[base : base + 16, k * 128 : (k + 1) * 128] = first.astype(jnp.bfloat16)
                    ycat[base + 16 : base + 32, k * 128 : (k + 1) * 128] = second.astype(jnp.bfloat16)
        spec_one[...] = jnp.dot(forward[...], xcat[...], preferred_element_type=jnp.float32)
        spec_two[...] = lax.dot_general(
            forward[...], ycat[...], (((1,), (1,)), ((), ())), preferred_element_type=jnp.float32
        )

        def mix(step, inner):
            cos_rows = pl.ds(step * 16, 16)
            sin_rows = pl.ds(FREQ + step * 16, 16)
            one_rr, one_ri = spec_one[cos_rows, 0:128], spec_one[cos_rows, 128:256]
            one_sr, one_si = spec_one[sin_rows, 0:128], spec_one[sin_rows, 128:256]
            two_rr, two_ri = spec_two[cos_rows, 0:128], spec_two[cos_rows, 128:256]
            two_sr, two_si = spec_two[sin_rows, 0:128], spec_two[sin_rows, 128:256]
            a_re, a_im = one_rr + one_si, one_ri - one_sr
            a_re_m, a_im_m = one_rr - one_si, one_ri + one_sr
            b_re, b_im = two_rr - two_si, two_ri + two_sr
            b_re_m, b_im_m = two_rr + two_si, two_ri - two_sr
            s_re = a_re * b_re - a_im * b_im
            s_im = a_re * b_im + a_im * b_re
            s_re_m = a_re_m * b_re_m - a_im_m * b_im_m
            s_im_m = a_re_m * b_im_m + a_im_m * b_re_m
            product[cos_rows, 0:128] = (s_re + s_re_m).astype(jnp.bfloat16)
            product[sin_rows, 0:128] = (s_im_m - s_im).astype(jnp.bfloat16)
            product[cos_rows, 128:256] = (s_im + s_im_m).astype(jnp.bfloat16)
            product[sin_rows, 128:256] = (s_re - s_re_m).astype(jnp.bfloat16)
            return inner

        lax.fori_loop(0, FREQ // 16, mix, 0)
        lagged = jnp.dot(inverse[...], product[...], preferred_element_type=jnp.float32)
        scale = 1.0 / (LENGTH * 32.0)
        pout[chunk, 0] = (scale * lagged[:, 128:256]).astype(jnp.bfloat16)
        pout[chunk, 1] = (-scale * lagged[:, 0:128]).astype(jnp.bfloat16)

    def apply_left(tiles, kind, side, column, parts=(0, 2)):
        def part(p, carry):
            swap[...] = tiles[pl.ds(4 * kind, 4), p].astype(jnp.float32).reshape(2048, 128)
            for pair in range(8):
                both = jnp.concatenate(
                    [
                        swap[pl.ds(2 * pair, 128, stride=16), :],
                        swap[pl.ds(2 * pair + 1, 128, stride=16), :],
                    ],
                    axis=1,
                ).astype(jnp.bfloat16)
                made = jnp.dot(left[side], both, preferred_element_type=jnp.float32)
                lower = pl.ds(256 * pair, 128)
                upper = pl.ds(256 * pair + 128, 128)
                total[p, column, lower, :] += made[:, 0:128]
                total[p, column, upper, :] += made[:, 128:256]
            return carry

        lax.fori_loop(*parts, part, 0)

    def finish_early(p, carry):
        def block(quad, inside):
            rows = pl.ds(quad * 512, 512)
            whole = jnp.concatenate([total[p, b, rows, :].astype(jnp.bfloat16) for b in range(5)], axis=1)
            for s in range(5):
                low, high = max(s - 1, 0) * 128, min(s + 2, 5) * 128
                made = jnp.dot(
                    whole[:, low:high],
                    right[low:high, s * 128 : s * 128 + 128],
                    preferred_element_type=jnp.float32,
                )
                for lag in range(4):
                    wide[p, s, pl.ds(quad * 4 + lag, 128, stride=16), :] = made[lag * 128 : lag * 128 + 128]
            return inside

        lax.fori_loop(0, 4, block, 0)
        for s in range(5):

            @pl.when((s < last - 1) | (s > last + 1))
            def _():
                out[p, 0, s] = wide[p, s].astype(jnp.bfloat16).reshape(128, 16, 128)

        return carry

    def finish_last(p, carry):
        swap[...] = nearby[pl.ds(8, 4), p].astype(jnp.float32).reshape(2048, 128)
        swap_two[...] = across[pl.ds(8, 4), p].astype(jnp.float32).reshape(2048, 128)
        both_left = jnp.concatenate([left[1 + toward], left[1 + inward]], axis=1)
        for pair in range(8):
            both = jnp.concatenate(
                [
                    jnp.concatenate(
                        [
                            held[pl.ds(2 * pair, 128, stride=16), :],
                            held[pl.ds(2 * pair + 1, 128, stride=16), :],
                        ],
                        axis=1,
                    )
                    for held in (swap, swap_two)
                ],
                axis=0,
            ).astype(jnp.bfloat16)
            made = jnp.dot(both_left, both, preferred_element_type=jnp.float32)
            lower = pl.ds(256 * pair, 128)
            upper = pl.ds(256 * pair + 128, 128)
            mixed[pl.ds(2 * pair, 128, stride=16), :] = made[:, 0:128] + total[p, last, lower, :]
            mixed[pl.ds(2 * pair + 1, 128, stride=16), :] = made[:, 128:256] + total[p, last, upper, :]
        for near in range(3):
            s = last + near - 1

            @pl.when((s >= 0) & (s < 5))
            def _():
                made = jnp.dot(
                    mixed[...].astype(jnp.bfloat16), right_last[near], preferred_element_type=jnp.float32
                )
                out[p, 0, s] = (wide[p, s] + made).astype(jnp.bfloat16).reshape(128, 16, 128)

        return carry

    send_x(jnp.int32(0))
    send_x(jnp.int32(1))
    load_diag.wait()
    turn(DIAG)
    send_y(jnp.int32(0))
    send_y(jnp.int32(1))

    @pl.when(is_outer)
    def _():
        bytes_of(graw.at[SHARED], sem_load.at[3])
        turn(SHARED)
        pltpu.make_async_copy(turned.at[SHARED, :, :, pl.ds(0, 32), :], ypass, sem_load.at[5]).start()
        remote(
            turned.at[SHARED, :, :, pl.ds(32, 32), :], ypass, sem_pass.at[2], sem_pass.at[3], across_rows(partner)
        ).start()

    place = lax.broadcasted_iota(jnp.int32, (128, 128), 1)
    orbital = lax.broadcasted_iota(jnp.int32, (128, 128), 0)
    order = (orbital == 4 * lax.rem(place, 32) + place // 32).astype(jnp.bfloat16)
    for side in range(3):
        left[side] = jnp.dot(coupling[row, side], order, preferred_element_type=jnp.float32).astype(jnp.bfloat16)
    for b in range(5):
        for s in range(max(b - 1, 0), min(b + 2, 5)):
            block = (slice(b * 128, b * 128 + 128), slice(s * 128, s * 128 + 128))
            tile_b, tile_c = row + b - 2, row + s - 2
            inside = (
                (tile_b >= 0) & (tile_b < 4) & (tile_c >= 0) & (tile_c < 4) & (b != last)
            ).astype(jnp.float32)
            safe = jnp.clip(tile_c, 0, 3)
            tile = coupling[safe, b - s + 1].astype(jnp.float32) * inside
            right[block] = tile.T.astype(jnp.bfloat16)

    for near in range(3):
        tile_b, tile_c = row + last - 2, row + last - 2 + near - 1
        inside = ((tile_c >= 0) & (tile_c < 4)).astype(jnp.float32)
        tile = coupling[jnp.clip(tile_c, 0, 3), 2 - near].astype(jnp.float32) * inside
        right_last[near] = tile.T.astype(jnp.bfloat16)

    @pl.when(is_outer)
    def _():
        for place in range(8, 12):
            across[place] = jnp.zeros((2, 32, 16, 128), jnp.bfloat16)

    def clear(step, carry):
        for b in range(5):
            total[0, b, pl.ds(step * 256, 256), :] = jnp.zeros((256, 128), jnp.float32)
            total[1, b, pl.ds(step * 256, 256), :] = jnp.zeros((256, 128), jnp.float32)
        return carry

    lax.fori_loop(0, 8, clear, 0)
    load_forward.wait()
    load_inverse.wait()


    def step(chunk, carry):
        arrive(chunk)
        correlate(chunk)
        send_p(chunk)
        ahead = chunk + AHEAD

        @pl.when(ahead == 4)
        def _():
            @pl.when(is_outer)
            def _():
                bytes_of(xpass, sem_pass.at[1])
                bytes_of(ypass, sem_load.at[5])

            @pl.when(is_inner)
            def _():
                bytes_of(xpass, sem_load.at[4])
                bytes_of(ypass, sem_pass.at[3])

        @pl.when(ahead == 6)
        def _():
            bytes_of(graw.at[INWARD], sem_raw.at[2])
            turn(INWARD)

        @pl.when(ahead < CHUNKS)
        def _():
            send_x(ahead)
            send_y(ahead)

        @pl.when(chunk >= 1)
        def _():
            gather(chunk - 1)

        @pl.when(chunk == 6)
        def _():
            apply_left(own, 0, 1, 2)

        @pl.when(chunk == 9)
        def _():
            for early in range(4):
                from_partner(early)
            apply_left(nearby, 0, 1 + toward, 2 + toward)

        return carry

    lax.fori_loop(0, CHUNKS, step, 0)

    @pl.when(is_inner)
    def _():
        for early in range(4):
            from_other(early)
        apply_left(across, 0, 1 + inward, 2 + inward)

    gather(jnp.int32(9))
    from_partner(4)
    from_partner(5)
    apply_left(own, 1, 1 + inward * (1 - inner), 2 - inward * inner)
    apply_left(own, 2, 1, 2 + inward)

    @pl.when(is_inner)
    def _():
        for chunk in range(4, 6):
            from_other(chunk)
            bytes_of(own.at[0], sem_far.at[1, chunk - 4])
        apply_left(across, 1, 1 + inward, 2 + 2 * inward)

    lax.fori_loop(0, 2, finish_early, 0)
    for chunk in range(6, CHUNKS):
        from_partner(chunk)

    @pl.when(is_inner)
    def _():
        for chunk in range(6, CHUNKS):
            from_other(chunk)

    lax.fori_loop(0, 2, finish_last, 0)
    @pl.when(is_inner)
    def _():
        bytes_of(xpass, sem_pass.at[0])
        bytes_of(graw.at[INWARD], sem_raw.at[0])
        bytes_of(graw.at[INWARD], sem_raw.at[1])

    @pl.when(is_outer)
    def _():
        bytes_of(ypass, sem_pass.at[2])
        for chunk in range(4, 6):
            bytes_of(own.at[0], sem_far.at[0, chunk - 4])

    def sent(chunk, carry):
        bytes_of(xin.at[chunk, :, pl.ds(0, 448), :], sem_x.at[0, chunk])
        bytes_of(yin.at[chunk, pl.ds(0, 31)], sem_y.at[0, chunk])
        bytes_of(own.at[0, :, pl.ds(0, 31)], sem_p.at[0, chunk])
        bytes_of(own.at[0], sem_near.at[0, chunk])

        @pl.when(is_inner)
        def _():
            bytes_of(own.at[0], sem_across.at[0, chunk])

        return carry

    lax.fori_loop(0, CHUNKS, sent, 0)


def shards(lesser, greater, coupling):
    forward, inverse = tables(512)
    half = jnp.bfloat16
    whole = jnp.float32
    anywhere = pl.BlockSpec(memory_space=pl.ANY)
    return pl.pallas_call(
        kernel,
        out_shape=pltpu.VMEM((2, 1, 5, 128, 16, 128), half),
        in_specs=[anywhere, anywhere, pl.BlockSpec(memory_space=pltpu.VMEM), anywhere, anywhere],
        out_specs=pl.BlockSpec(memory_space=pltpu.VMEM),
        scratch_shapes=[
            pltpu.VMEM((LENGTH, 512), half),
            pltpu.VMEM((512, LENGTH), half),
            pltpu.VMEM((3, 2, 32, 64, 128), half),
            pltpu.VMEM((3, 2, 32, 64, 128), half),
            pltpu.VMEM((2, 8, 2, 64, 128), half),
            pltpu.VMEM((2, 32, 32, 128), half),
            pltpu.VMEM((CHUNKS, 2, 512, 128), half),
            pltpu.VMEM((CHUNKS, 32, 2, 16, 128), half),
            pltpu.VMEM((CHUNKS, 2, 512, 128), half),
            pltpu.VMEM((12, 2, 32, 16, 128), half),
            pltpu.VMEM((12, 2, 32, 16, 128), half),
            pltpu.VMEM((12, 2, 32, 16, 128), half),
            pltpu.VMEM((2, 5, 2048, 128), whole),
            pltpu.VMEM((2048, 128), whole),
            pltpu.VMEM((2048, 128), whole),
            pltpu.VMEM((2048, 128), whole),
            pltpu.VMEM((2, 5, 2048, 128), whole),
            pltpu.VMEM((3, 128, 128), half),
            pltpu.VMEM((640, 640), half),
            pltpu.VMEM((3, 128, 128), half),
            pltpu.VMEM((512, 256), half),
            pltpu.VMEM((256, 512), half),
            pltpu.VMEM((LENGTH, 256), whole),
            pltpu.VMEM((LENGTH, 256), whole),
            pltpu.VMEM((LENGTH, 256), half),
            pltpu.SemaphoreType.DMA((6,)),
            pltpu.SemaphoreType.DMA((3, CHUNKS)),
            pltpu.SemaphoreType.DMA((3,)),
            pltpu.SemaphoreType.DMA((4,)),
            pltpu.SemaphoreType.DMA((2, CHUNKS)),
            pltpu.SemaphoreType.DMA((2, CHUNKS)),
            pltpu.SemaphoreType.DMA((2, CHUNKS)),
            pltpu.SemaphoreType.DMA((2, CHUNKS)),
            pltpu.SemaphoreType.DMA((2, CHUNKS)),
            pltpu.SemaphoreType.DMA((2, 2)),
        ],
        compiler_params=pltpu.CompilerParams(
            collective_id=0, has_side_effects=True, vmem_limit_bytes=55 * 1024 * 1024
        ),
        cost_estimate=pl.CostEstimate(flops=10**10, bytes_accessed=2 * 10**7, transcendentals=0),
    )(
        lesser.reshape(2, 3, 8, 4, 64, 128),
        greater.reshape(2, 3, 32, 64, 128),
        coupling,
        jnp.asarray(forward),
        jnp.asarray(inverse),
    )


def solution(mesh):
    placed = (P(None, "row", None, "col", "en", None), P(None, "row", None, "col", "en", None), P())
    return jax.shard_map(
        shards,
        mesh=mesh,
        in_specs=placed,
        out_specs=P(None, "row", None, None, ("col", "en"), None),
        check_vma=False,
    )
```

```python
import math

import jax
import jax.numpy as jnp
import ml_dtypes
import numpy as np
from jax import lax
from jax.experimental import pallas as pl
from jax.experimental.pallas import tpu as pltpu
from jax.sharding import PartitionSpec as P

MESH = pl.DeviceIdType.MESH
DIAG, INWARD, SHARED = 0, 1, 2
FREQ = 384
LENGTH = 2 * FREQ


def tables(energies):
    freq = 2 * np.arange(FREQ)[:, None] + 1
    ahead = freq * np.arange(energies)[None, :] % (2 * LENGTH)
    back = (np.arange(energies) - energies // 2)[:, None] * freq.T % (2 * LENGTH)
    ahead = ahead * (math.pi / LENGTH)
    back = back * (math.pi / LENGTH)
    forward = np.concatenate([np.cos(ahead), np.sin(ahead)], axis=0)
    inverse = np.concatenate([np.cos(back), np.sin(back)], axis=1)
    return forward.astype(ml_dtypes.bfloat16), inverse.astype(ml_dtypes.bfloat16)


CHUNKS = 10
AHEAD = 2


def kernel(
    lesser,
    greater,
    coupling,
    forward_hbm,
    inverse_hbm,
    out,
    forward,
    inverse,
    graw,
    turned,
    xpass,
    ypass,
    xin,
    yin,
    pout,
    own,
    nearby,
    across,
    total,
    swap,
    swap_two,
    mixed,
    wide,
    left,
    right,
    right_last,
    xcat,
    ycat,
    spec_one,
    spec_two,
    product,
    sem_load,
    sem_keep,
    sem_raw,
    sem_pass,
    sem_x,
    sem_y,
    sem_p,
    sem_near,
    sem_across,
    sem_far,
):
    row = lax.axis_index("row")
    col = lax.axis_index("col")
    en = lax.axis_index("en")
    me = col * 8 + en
    partner = row + 1 - 2 * lax.rem(row, 2)
    other = 3 - row
    far = lax.rem(row + 2, 4)
    inward = 1 - 2 * (row // 2)
    inner = lax.rem(lax.rem(row, 2) + row // 2, 2)
    is_inner = inner == 1
    is_outer = inner == 0
    slot_in, slot_out = 1 + inward, 1 - inward
    toward = inward * (1 - 2 * inner)
    last = 2 + 2 * inward * (1 - inner)

    def peer(step):
        index = lax.rem(me + step, 32)
        return index, (row, index // 8, lax.rem(index, 8))

    def remote(src, dst, send, recv, target):
        return pltpu.make_async_remote_copy(
            src_ref=src,
            dst_ref=dst,
            send_sem=send,
            recv_sem=recv,
            device_id=target,
            device_id_type=MESH,
        )

    def across_rows(target):
        return (target, col, en)

    def bytes_of(ref, sem):
        pltpu.make_async_copy(ref, ref, sem).wait()

    load_diag = pltpu.make_async_copy(greater.at[:, 1], graw.at[DIAG], sem_load.at[0])
    load_forward = pltpu.make_async_copy(forward_hbm, forward, sem_load.at[1])
    load_inverse = pltpu.make_async_copy(inverse_hbm, inverse, sem_load.at[2])
    load_diag.start()

    @pl.when(is_outer)
    def _():
        pltpu.make_async_copy(greater.at[:, slot_in], graw.at[SHARED], sem_load.at[3]).start()

    @pl.when(is_inner)
    def _():
        pltpu.make_async_copy(lesser.at[:, slot_out, :, pl.ds(2, 2)], xpass, sem_load.at[4]).start()

    load_forward.start()
    load_inverse.start()

    barrier = pltpu.get_barrier_semaphore()

    def greet(step, carry):
        pl.semaphore_signal(barrier, inc=1, device_id=peer(step)[1], device_id_type=MESH)
        return carry

    lax.fori_loop(1, 32, greet, 0)
    for step in range(1, 4):
        pl.semaphore_signal(
            barrier, inc=1, device_id=across_rows(lax.rem(row + step, 4)), device_id_type=MESH
        )
    pl.semaphore_wait(barrier, 34)

    @pl.when(is_inner)
    def _():
        remote(
            lesser.at[:, slot_out, :, pl.ds(0, 2)], xpass, sem_pass.at[0], sem_pass.at[1], across_rows(partner)
        ).start()
        remote(
            greater.at[:, slot_out], graw.at[INWARD], sem_raw.at[0], sem_raw.at[2], across_rows(partner)
        ).start()
        remote(
            greater.at[:, slot_in], graw.at[INWARD], sem_raw.at[1], sem_raw.at[2], across_rows(other)
        ).start()

    def is_kind(chunk, kind):
        if kind == DIAG:
            return chunk < 4
        if kind == SHARED:
            return (chunk >= 4) & (chunk < 6)
        return chunk >= 6

    def place_of(chunk):
        shared = (chunk >= 4).astype(jnp.int32) - (chunk >= 6).astype(jnp.int32)
        return chunk + 2 * inner * shared + 2 * (chunk >= 6).astype(jnp.int32)

    def send_x(chunk):
        place = xin.at[chunk, :, pl.ds(64 * en, 64), :]

        def spread(source):
            def body(step, carry):
                to = lax.rem(en + step, 8)
                remote(source(to), place, sem_x.at[0, chunk], sem_x.at[1, chunk], (row, col, to)).start()
                return carry

            lax.fori_loop(1, 8, body, 0)
            pltpu.make_async_copy(source(en), place, sem_keep.at[0, chunk]).start()

        @pl.when(is_kind(chunk, SHARED))
        def _():
            spread(lambda to: xpass.at[:, to, chunk - 4])

        @pl.when(jnp.logical_not(is_kind(chunk, SHARED)))
        def _():
            inside = (chunk >= 6).astype(jnp.int32)
            spread(lambda to: lesser.at[:, 1 + inside * inward, to, chunk - 6 * inside])

    def send_y(chunk):
        place = yin.at[chunk, me]

        def spread(source):
            def body(step, carry):
                index, target = peer(step)
                remote(source(index), place, sem_y.at[0, chunk], sem_y.at[1, chunk], target).start()
                return carry

            lax.fori_loop(1, 32, body, 0)
            pltpu.make_async_copy(source(me), place, sem_keep.at[1, chunk]).start()

        @pl.when(is_kind(chunk, SHARED))
        def _():
            spread(lambda index: ypass.at[:, index, pl.ds(16 * (chunk - 4), 16), :])

        @pl.when(jnp.logical_not(is_kind(chunk, SHARED)))
        def _():
            inside = (chunk >= 6).astype(jnp.int32)
            spread(lambda index: turned.at[inside, :, index, pl.ds(16 * (chunk - 6 * inside), 16), :])

    def send_p(chunk):
        place = own.at[place_of(chunk), :, me]

        def body(step, carry):
            index, target = peer(step)
            remote(
                pout.at[chunk, :, pl.ds(16 * index, 16), :], place, sem_p.at[0, chunk], sem_p.at[1, chunk], target
            ).start()
            return carry

        lax.fori_loop(1, 32, body, 0)
        pltpu.make_async_copy(pout.at[chunk, :, pl.ds(16 * me, 16), :], place, sem_keep.at[2, chunk]).start()

    def arrive(chunk):
        bytes_of(xin.at[chunk, :, pl.ds(0, 448), :], sem_x.at[1, chunk])
        bytes_of(xin.at[chunk, :, pl.ds(0, 64), :], sem_keep.at[0, chunk])
        bytes_of(yin.at[chunk, pl.ds(0, 31)], sem_y.at[1, chunk])
        bytes_of(yin.at[chunk, 0], sem_keep.at[1, chunk])

    def gather(chunk):
        bytes_of(own.at[0, :, pl.ds(0, 31)], sem_p.at[1, chunk])
        bytes_of(own.at[0, :, 0], sem_keep.at[2, chunk])
        place = place_of(chunk)
        src = own.at[place]

        def to_partner(dst):
            remote(
                src, dst.at[place], sem_near.at[0, chunk], sem_near.at[1, chunk], across_rows(partner)
            ).start()

        @pl.when(is_kind(chunk, SHARED))
        def _():
            to_partner(own)

        @pl.when(jnp.logical_not(is_kind(chunk, SHARED)))
        def _():
            to_partner(nearby)

        @pl.when(is_inner)
        def _():
            remote(
                src, across.at[place], sem_across.at[0, chunk], sem_across.at[1, chunk], across_rows(other)
            ).start()

        @pl.when(is_outer & is_kind(chunk, SHARED))
        def _():
            remote(
                src, across.at[place], sem_far.at[0, chunk - 4], sem_far.at[1, chunk - 4], across_rows(far)
            ).start()

    def gather_last():
        chunk = CHUNKS - 1
        bytes_of(own.at[0, :, pl.ds(0, 31)], sem_p.at[1, chunk])
        bytes_of(own.at[0, :, 0], sem_keep.at[2, chunk])
        place = chunk + 2
        for p in range(2):
            remote(
                own.at[place, p],
                nearby.at[place, p],
                sem_near.at[0, chunk + p],
                sem_near.at[1, chunk + p],
                across_rows(partner),
            ).start()

            @pl.when(is_inner)
            def _():
                remote(
                    own.at[place, p],
                    across.at[place, p],
                    sem_across.at[0, chunk + p],
                    sem_across.at[1, chunk + p],
                    across_rows(other),
                ).start()

    def from_partner(chunk):
        bytes_of(own.at[0], sem_near.at[1, chunk])

    def from_other(chunk):
        bytes_of(own.at[0], sem_across.at[1, chunk])

    def turn(kind):
        def part(p, carry):
            def one(s, inside):
                square = jnp.concatenate([graw[kind, p, s], graw[kind, p, s + 16]], axis=0).astype(jnp.float32)
                swap[pl.ds(s, 128, stride=16), :] = square.T
                return inside

            lax.fori_loop(0, 16, one, 0)
            turned[kind, p] = swap[...].astype(jnp.bfloat16).reshape(32, 64, 128)
            return carry

        lax.fori_loop(0, 2, part, 0)

    lane = lax.broadcasted_iota(jnp.int32, (16, 128), 1)

    def correlate(chunk):
        for p in range(2):
            xcat[:, p * 128 : (p + 1) * 128] = xin[chunk, p]
        for p in range(2):
            for c in range(4):
                for k in range(4):
                    one = yin[chunk, c * 8 + 2 * k, p].astype(jnp.float32)
                    two = yin[chunk, c * 8 + 2 * k + 1, p].astype(jnp.float32)
                    first = jnp.where(lane < 64, one, pltpu.roll(two, 64, 1))
                    second = jnp.where(lane < 64, pltpu.roll(one, 64, 1), two)
                    base = p * 128 + c * 32
                    ycat[base : base + 16, k * 128 : (k + 1) * 128] = first.astype(jnp.bfloat16)
                    ycat[base + 16 : base + 32, k * 128 : (k + 1) * 128] = second.astype(jnp.bfloat16)
        spec_one[...] = jnp.dot(forward[...], xcat[...], preferred_element_type=jnp.float32)
        spec_two[...] = lax.dot_general(
            forward[...], ycat[...], (((1,), (1,)), ((), ())), preferred_element_type=jnp.float32
        )

        def mix(step, inner):
            cos_rows = pl.ds(step * 16, 16)
            sin_rows = pl.ds(FREQ + step * 16, 16)
            one_rr, one_ri = spec_one[cos_rows, 0:128], spec_one[cos_rows, 128:256]
            one_sr, one_si = spec_one[sin_rows, 0:128], spec_one[sin_rows, 128:256]
            two_rr, two_ri = spec_two[cos_rows, 0:128], spec_two[cos_rows, 128:256]
            two_sr, two_si = spec_two[sin_rows, 0:128], spec_two[sin_rows, 128:256]
            a_re, a_im = one_rr + one_si, one_ri - one_sr
            a_re_m, a_im_m = one_rr - one_si, one_ri + one_sr
            b_re, b_im = two_rr - two_si, two_ri + two_sr
            b_re_m, b_im_m = two_rr + two_si, two_ri - two_sr
            s_re = a_re * b_re - a_im * b_im
            s_im = a_re * b_im + a_im * b_re
            s_re_m = a_re_m * b_re_m - a_im_m * b_im_m
            s_im_m = a_re_m * b_im_m + a_im_m * b_re_m
            product[cos_rows, 0:128] = (s_re + s_re_m).astype(jnp.bfloat16)
            product[sin_rows, 0:128] = (s_im_m - s_im).astype(jnp.bfloat16)
            product[cos_rows, 128:256] = (s_im + s_im_m).astype(jnp.bfloat16)
            product[sin_rows, 128:256] = (s_re - s_re_m).astype(jnp.bfloat16)
            return inner

        lax.fori_loop(0, FREQ // 16, mix, 0, unroll=4)
        lagged = jnp.dot(inverse[...], product[...], preferred_element_type=jnp.float32)
        scale = 1.0 / (LENGTH * 32.0)
        pout[chunk, 0] = (scale * lagged[:, 128:256]).astype(jnp.bfloat16)
        pout[chunk, 1] = (-scale * lagged[:, 0:128]).astype(jnp.bfloat16)

    def apply_left(tiles, kind, side, column, parts=(0, 2)):
        def part(p, carry):
            swap[...] = tiles[pl.ds(4 * kind, 4), p].astype(jnp.float32).reshape(2048, 128)
            for pair in range(8):
                both = jnp.concatenate(
                    [
                        swap[pl.ds(2 * pair, 128, stride=16), :],
                        swap[pl.ds(2 * pair + 1, 128, stride=16), :],
                    ],
                    axis=1,
                ).astype(jnp.bfloat16)
                made = jnp.dot(left[side], both, preferred_element_type=jnp.float32)
                lower = pl.ds(256 * pair, 128)
                upper = pl.ds(256 * pair + 128, 128)
                total[p, column, lower, :] += made[:, 0:128]
                total[p, column, upper, :] += made[:, 128:256]
            return carry

        lax.fori_loop(*parts, part, 0)

    def finish_early(p, carry):
        def block(quad, inside):
            rows = pl.ds(quad * 512, 512)
            whole = jnp.concatenate([total[p, b, rows, :].astype(jnp.bfloat16) for b in range(5)], axis=1)
            for first, count, low, high in ((0, 2, 0, 384), (2, 2, 128, 640), (4, 1, 384, 640)):
                made = jnp.dot(
                    whole[:, low:high],
                    right[low:high, first * 128 : (first + count) * 128],
                    preferred_element_type=jnp.float32,
                )
                for s in range(first, first + count):
                    for lag in range(4):
                        wide[p, s, pl.ds(quad * 4 + lag, 128, stride=16), :] = made[
                            lag * 128 : lag * 128 + 128, (s - first) * 128 : (s - first) * 128 + 128
                        ]
            return inside

        lax.fori_loop(0, 4, block, 0)
        for s in range(5):

            @pl.when((s < last - 1) | (s > last + 1))
            def _():
                out[p, 0, s] = wide[p, s].astype(jnp.bfloat16).reshape(128, 16, 128)

        return carry

    def finish_last(p, carry):
        bytes_of(own.at[0, 0], sem_near.at[1, CHUNKS - 1 + p])

        @pl.when(is_inner)
        def _():
            bytes_of(own.at[0, 0], sem_across.at[1, CHUNKS - 1 + p])

        swap[...] = nearby[pl.ds(8, 4), p].astype(jnp.float32).reshape(2048, 128)
        swap_two[...] = across[pl.ds(8, 4), p].astype(jnp.float32).reshape(2048, 128)
        both_left = jnp.concatenate([left[1 + toward], left[1 + inward]], axis=1)
        for pair in range(8):
            both = jnp.concatenate(
                [
                    jnp.concatenate(
                        [
                            held[pl.ds(2 * pair, 128, stride=16), :],
                            held[pl.ds(2 * pair + 1, 128, stride=16), :],
                        ],
                        axis=1,
                    )
                    for held in (swap, swap_two)
                ],
                axis=0,
            ).astype(jnp.bfloat16)
            made = jnp.dot(both_left, both, preferred_element_type=jnp.float32)
            lower = pl.ds(256 * pair, 128)
            upper = pl.ds(256 * pair + 128, 128)
            mixed[pl.ds(2 * pair, 128, stride=16), :] = made[:, 0:128] + total[p, last, lower, :]
            mixed[pl.ds(2 * pair + 1, 128, stride=16), :] = made[:, 128:256] + total[p, last, upper, :]
        for near in range(3):
            s = last + near - 1

            @pl.when((s >= 0) & (s < 5))
            def _():
                made = jnp.dot(
                    mixed[...].astype(jnp.bfloat16), right_last[near], preferred_element_type=jnp.float32
                )
                out[p, 0, s] = (wide[p, s] + made).astype(jnp.bfloat16).reshape(128, 16, 128)

        return carry

    send_x(jnp.int32(0))
    send_x(jnp.int32(1))
    load_diag.wait()
    turn(DIAG)
    send_y(jnp.int32(0))
    send_y(jnp.int32(1))

    @pl.when(is_outer)
    def _():
        bytes_of(graw.at[SHARED], sem_load.at[3])
        turn(SHARED)
        pltpu.make_async_copy(turned.at[SHARED, :, :, pl.ds(0, 32), :], ypass, sem_load.at[5]).start()
        remote(
            turned.at[SHARED, :, :, pl.ds(32, 32), :], ypass, sem_pass.at[2], sem_pass.at[3], across_rows(partner)
        ).start()

    place = lax.broadcasted_iota(jnp.int32, (128, 128), 1)
    orbital = lax.broadcasted_iota(jnp.int32, (128, 128), 0)
    order = (orbital == 4 * lax.rem(place, 32) + place // 32).astype(jnp.bfloat16)
    for side in range(3):
        left[side] = jnp.dot(coupling[row, side], order, preferred_element_type=jnp.float32).astype(jnp.bfloat16)
    for b, s in ((2, 0), (1, 3), (4, 2)):
        right[b * 128 : b * 128 + 128, s * 128 : s * 128 + 128] = jnp.zeros((128, 128), jnp.bfloat16)
    for b in range(5):
        for s in range(max(b - 1, 0), min(b + 2, 5)):
            block = (slice(b * 128, b * 128 + 128), slice(s * 128, s * 128 + 128))
            tile_b, tile_c = row + b - 2, row + s - 2
            inside = (
                (tile_b >= 0) & (tile_b < 4) & (tile_c >= 0) & (tile_c < 4) & (b != last)
            ).astype(jnp.float32)
            safe = jnp.clip(tile_c, 0, 3)
            tile = coupling[safe, b - s + 1].astype(jnp.float32) * inside
            right[block] = tile.T.astype(jnp.bfloat16)

    for near in range(3):
        tile_b, tile_c = row + last - 2, row + last - 2 + near - 1
        inside = ((tile_c >= 0) & (tile_c < 4)).astype(jnp.float32)
        tile = coupling[jnp.clip(tile_c, 0, 3), 2 - near].astype(jnp.float32) * inside
        right_last[near] = tile.T.astype(jnp.bfloat16)

    @pl.when(is_outer)
    def _():
        for place in range(8, 12):
            across[place] = jnp.zeros((2, 32, 16, 128), jnp.bfloat16)

    def clear(step, carry):
        for b in range(5):
            total[0, b, pl.ds(step * 256, 256), :] = jnp.zeros((256, 128), jnp.float32)
            total[1, b, pl.ds(step * 256, 256), :] = jnp.zeros((256, 128), jnp.float32)
        return carry

    lax.fori_loop(0, 8, clear, 0)
    load_forward.wait()
    load_inverse.wait()


    def step(chunk, carry):
        arrive(chunk)
        ahead = chunk + AHEAD

        @pl.when(ahead < 4)
        def _():
            send_x(ahead)

        @pl.when((ahead > 6) & (ahead < CHUNKS))
        def _():
            send_x(ahead)

        correlate(chunk)
        send_p(chunk)

        @pl.when(ahead == 4)
        def _():
            @pl.when(is_outer)
            def _():
                bytes_of(xpass, sem_pass.at[1])
                bytes_of(ypass, sem_load.at[5])

            @pl.when(is_inner)
            def _():
                bytes_of(xpass, sem_load.at[4])
                bytes_of(ypass, sem_pass.at[3])

        @pl.when(ahead == 6)
        def _():
            bytes_of(graw.at[INWARD], sem_raw.at[2])
            turn(INWARD)

        @pl.when(ahead < CHUNKS)
        def _():
            @pl.when((ahead >= 4) & (ahead <= 6))
            def _():
                send_x(ahead)

            send_y(ahead)

        @pl.when(chunk >= 1)
        def _():
            gather(chunk - 1)

        @pl.when(chunk == 6)
        def _():
            apply_left(own, 0, 1, 2)

        @pl.when(chunk == 7)
        def _():
            for early in range(4):
                from_partner(early)
            apply_left(nearby, 0, 1 + toward, 2 + toward)

        @pl.when((chunk == 8) & is_inner)
        def _():
            for early in range(4):
                from_other(early)
            apply_left(across, 0, 1 + inward, 2 + inward)

        return carry

    lax.fori_loop(0, CHUNKS, step, 0)

    from_partner(4)
    from_partner(5)
    apply_left(own, 1, 1 + inward * (1 - inner), 2 - inward * inner)
    gather_last()
    apply_left(own, 2, 1, 2 + inward)

    @pl.when(is_inner)
    def _():
        for chunk in range(4, 6):
            from_other(chunk)
            bytes_of(own.at[0], sem_far.at[1, chunk - 4])
        apply_left(across, 1, 1 + inward, 2 + 2 * inward)

    lax.fori_loop(0, 2, finish_early, 0)
    for chunk in range(6, CHUNKS - 1):
        from_partner(chunk)

    @pl.when(is_inner)
    def _():
        for chunk in range(6, CHUNKS - 1):
            from_other(chunk)

    lax.fori_loop(0, 2, finish_last, 0)
    @pl.when(is_inner)
    def _():
        bytes_of(xpass, sem_pass.at[0])
        bytes_of(graw.at[INWARD], sem_raw.at[0])
        bytes_of(graw.at[INWARD], sem_raw.at[1])

    @pl.when(is_outer)
    def _():
        bytes_of(ypass, sem_pass.at[2])
        for chunk in range(4, 6):
            bytes_of(own.at[0], sem_far.at[0, chunk - 4])

    def sent(chunk, carry):
        bytes_of(xin.at[chunk, :, pl.ds(0, 448), :], sem_x.at[0, chunk])
        bytes_of(yin.at[chunk, pl.ds(0, 31)], sem_y.at[0, chunk])
        bytes_of(own.at[0, :, pl.ds(0, 31)], sem_p.at[0, chunk])
        return carry

    def passed_on(chunk, carry):
        bytes_of(own.at[0], sem_near.at[0, chunk])

        @pl.when(is_inner)
        def _():
            bytes_of(own.at[0], sem_across.at[0, chunk])

        return carry

    lax.fori_loop(0, CHUNKS, sent, 0)
    lax.fori_loop(0, CHUNKS - 1, passed_on, 0)
    for p in range(2):
        bytes_of(own.at[0, 0], sem_near.at[0, CHUNKS - 1 + p])

        @pl.when(is_inner)
        def _():
            bytes_of(own.at[0, 0], sem_across.at[0, CHUNKS - 1 + p])


def shards(lesser, greater, coupling):
    forward, inverse = tables(512)
    half = jnp.bfloat16
    whole = jnp.float32
    anywhere = pl.BlockSpec(memory_space=pl.ANY)
    return pl.pallas_call(
        kernel,
        out_shape=pltpu.VMEM((2, 1, 5, 128, 16, 128), half),
        in_specs=[anywhere, anywhere, pl.BlockSpec(memory_space=pltpu.VMEM), anywhere, anywhere],
        out_specs=pl.BlockSpec(memory_space=pltpu.VMEM),
        scratch_shapes=[
            pltpu.VMEM((LENGTH, 512), half),
            pltpu.VMEM((512, LENGTH), half),
            pltpu.VMEM((3, 2, 32, 64, 128), half),
            pltpu.VMEM((3, 2, 32, 64, 128), half),
            pltpu.VMEM((2, 8, 2, 64, 128), half),
            pltpu.VMEM((2, 32, 32, 128), half),
            pltpu.VMEM((CHUNKS, 2, 512, 128), half),
            pltpu.VMEM((CHUNKS, 32, 2, 16, 128), half),
            pltpu.VMEM((CHUNKS, 2, 512, 128), half),
            pltpu.VMEM((12, 2, 32, 16, 128), half),
            pltpu.VMEM((12, 2, 32, 16, 128), half),
            pltpu.VMEM((12, 2, 32, 16, 128), half),
            pltpu.VMEM((2, 5, 2048, 128), whole),
            pltpu.VMEM((2048, 128), whole),
            pltpu.VMEM((2048, 128), whole),
            pltpu.VMEM((2048, 128), whole),
            pltpu.VMEM((2, 5, 2048, 128), whole),
            pltpu.VMEM((3, 128, 128), half),
            pltpu.VMEM((640, 640), half),
            pltpu.VMEM((3, 128, 128), half),
            pltpu.VMEM((512, 256), half),
            pltpu.VMEM((256, 512), half),
            pltpu.VMEM((LENGTH, 256), whole),
            pltpu.VMEM((LENGTH, 256), whole),
            pltpu.VMEM((LENGTH, 256), half),
            pltpu.SemaphoreType.DMA((6,)),
            pltpu.SemaphoreType.DMA((3, CHUNKS)),
            pltpu.SemaphoreType.DMA((3,)),
            pltpu.SemaphoreType.DMA((4,)),
            pltpu.SemaphoreType.DMA((2, CHUNKS)),
            pltpu.SemaphoreType.DMA((2, CHUNKS)),
            pltpu.SemaphoreType.DMA((2, CHUNKS)),
            pltpu.SemaphoreType.DMA((2, CHUNKS + 1)),
            pltpu.SemaphoreType.DMA((2, CHUNKS + 1)),
            pltpu.SemaphoreType.DMA((2, 2)),
        ],
        compiler_params=pltpu.CompilerParams(
            collective_id=0, has_side_effects=True, vmem_limit_bytes=55 * 1024 * 1024
        ),
        cost_estimate=pl.CostEstimate(flops=10**10, bytes_accessed=2 * 10**7, transcendentals=0),
    )(
        lesser.reshape(2, 3, 8, 4, 64, 128),
        greater.reshape(2, 3, 32, 64, 128),
        coupling,
        jnp.asarray(forward),
        jnp.asarray(inverse),
    )


def solution(mesh):
    placed = (P(None, "row", None, "col", "en", None), P(None, "row", None, "col", "en", None), P())
    return jax.shard_map(
        shards,
        mesh=mesh,
        in_specs=placed,
        out_specs=P(None, "row", None, None, ("col", "en"), None),
        check_vma=False,
    )
```

```python
import math

import jax
import jax.numpy as jnp
import ml_dtypes
import numpy as np
from jax import lax
from jax.experimental import pallas as pl
from jax.experimental.pallas import tpu as pltpu
from jax.sharding import PartitionSpec as P

MESH = pl.DeviceIdType.MESH
DIAG, INWARD, SHARED = 0, 1, 2
FREQ = 384
LENGTH = 2 * FREQ


def tables(energies):
    freq = 2 * np.arange(FREQ)[:, None] + 1
    ahead = freq * np.arange(energies)[None, :] % (2 * LENGTH)
    back = (np.arange(energies) - energies // 2)[:, None] * freq.T % (2 * LENGTH)
    ahead = ahead * (math.pi / LENGTH)
    back = back * (math.pi / LENGTH)
    forward = np.concatenate([np.cos(ahead), np.sin(ahead)], axis=0)
    inverse = np.concatenate([np.cos(back), np.sin(back)], axis=1)
    return forward.astype(ml_dtypes.bfloat16), inverse.astype(ml_dtypes.bfloat16)


CHUNKS = 10
AHEAD = 2


def kernel(
    lesser,
    greater,
    coupling,
    forward_hbm,
    inverse_hbm,
    out,
    forward,
    inverse,
    graw,
    turned,
    xpass,
    ypass,
    xin,
    yin,
    pout,
    own,
    nearby,
    across,
    total,
    swap,
    swap_two,
    mixed,
    wide,
    left,
    right,
    right_last,
    xcat,
    ycat,
    spec_one,
    spec_two,
    product,
    sem_load,
    sem_keep,
    sem_raw,
    sem_pass,
    sem_x,
    sem_y,
    sem_p,
    sem_near,
    sem_across,
    sem_far,
):
    row = lax.axis_index("row")
    col = lax.axis_index("col")
    en = lax.axis_index("en")
    me = col * 8 + en
    partner = row + 1 - 2 * lax.rem(row, 2)
    other = 3 - row
    far = lax.rem(row + 2, 4)
    inward = 1 - 2 * (row // 2)
    inner = lax.rem(lax.rem(row, 2) + row // 2, 2)
    is_inner = inner == 1
    is_outer = inner == 0
    slot_in, slot_out = 1 + inward, 1 - inward
    toward = inward * (1 - 2 * inner)
    last = 2 + 2 * inward * (1 - inner)

    def peer(step):
        index = lax.rem(me + step, 32)
        return index, (row, index // 8, lax.rem(index, 8))

    def remote(src, dst, send, recv, target):
        return pltpu.make_async_remote_copy(
            src_ref=src,
            dst_ref=dst,
            send_sem=send,
            recv_sem=recv,
            device_id=target,
            device_id_type=MESH,
        )

    def across_rows(target):
        return (target, col, en)

    def bytes_of(ref, sem):
        pltpu.make_async_copy(ref, ref, sem).wait()

    load_diag = pltpu.make_async_copy(greater.at[:, 1], graw.at[DIAG], sem_load.at[0])
    load_forward = pltpu.make_async_copy(forward_hbm, forward, sem_load.at[1])
    load_inverse = pltpu.make_async_copy(inverse_hbm, inverse, sem_load.at[2])
    load_diag.start()

    @pl.when(is_outer)
    def _():
        pltpu.make_async_copy(greater.at[:, slot_in], graw.at[SHARED], sem_load.at[3]).start()

    @pl.when(is_inner)
    def _():
        pltpu.make_async_copy(lesser.at[:, slot_out, :, pl.ds(2, 2)], xpass, sem_load.at[4]).start()

    load_forward.start()
    load_inverse.start()

    barrier = pltpu.get_barrier_semaphore()

    def greet(step, carry):
        pl.semaphore_signal(barrier, inc=1, device_id=peer(step)[1], device_id_type=MESH)
        return carry

    lax.fori_loop(1, 32, greet, 0)
    for step in range(1, 4):
        pl.semaphore_signal(
            barrier, inc=1, device_id=across_rows(lax.rem(row + step, 4)), device_id_type=MESH
        )
    pl.semaphore_wait(barrier, 34)

    @pl.when(is_inner)
    def _():
        remote(
            lesser.at[:, slot_out, :, pl.ds(0, 2)], xpass, sem_pass.at[0], sem_pass.at[1], across_rows(partner)
        ).start()
        remote(
            greater.at[:, slot_out], graw.at[INWARD], sem_raw.at[0], sem_raw.at[2], across_rows(partner)
        ).start()
        remote(
            greater.at[:, slot_in], graw.at[INWARD], sem_raw.at[1], sem_raw.at[2], across_rows(other)
        ).start()

    def is_kind(chunk, kind):
        if kind == DIAG:
            return chunk < 4
        if kind == SHARED:
            return (chunk >= 4) & (chunk < 6)
        return chunk >= 6

    def place_of(chunk):
        shared = (chunk >= 4).astype(jnp.int32) - (chunk >= 6).astype(jnp.int32)
        return chunk + 2 * inner * shared + 2 * (chunk >= 6).astype(jnp.int32)

    def send_x(chunk):
        place = xin.at[chunk, :, pl.ds(64 * en, 64), :]

        def spread(source):
            def body(step, carry):
                to = lax.rem(en + step, 8)
                remote(source(to), place, sem_x.at[0, chunk], sem_x.at[1, chunk], (row, col, to)).start()
                return carry

            lax.fori_loop(1, 8, body, 0)
            pltpu.make_async_copy(source(en), place, sem_keep.at[0, chunk]).start()

        @pl.when(is_kind(chunk, SHARED))
        def _():
            spread(lambda to: xpass.at[:, to, chunk - 4])

        @pl.when(jnp.logical_not(is_kind(chunk, SHARED)))
        def _():
            inside = (chunk >= 6).astype(jnp.int32)
            spread(lambda to: lesser.at[:, 1 + inside * inward, to, chunk - 6 * inside])

    def send_y(chunk):
        place = yin.at[chunk, me]

        def spread(source):
            def body(step, carry):
                index, target = peer(step)
                remote(source(index), place, sem_y.at[0, chunk], sem_y.at[1, chunk], target).start()
                return carry

            lax.fori_loop(1, 32, body, 0)
            pltpu.make_async_copy(source(me), place, sem_keep.at[1, chunk]).start()

        @pl.when(is_kind(chunk, SHARED))
        def _():
            spread(lambda index: ypass.at[:, index, pl.ds(16 * (chunk - 4), 16), :])

        @pl.when(jnp.logical_not(is_kind(chunk, SHARED)))
        def _():
            inside = (chunk >= 6).astype(jnp.int32)
            spread(lambda index: turned.at[inside, :, index, pl.ds(16 * (chunk - 6 * inside), 16), :])

    def send_p(chunk):
        place = own.at[place_of(chunk), :, me]

        def body(step, carry):
            index, target = peer(step)
            remote(
                pout.at[chunk, :, pl.ds(16 * index, 16), :], place, sem_p.at[0, chunk], sem_p.at[1, chunk], target
            ).start()
            return carry

        lax.fori_loop(1, 32, body, 0)
        pltpu.make_async_copy(pout.at[chunk, :, pl.ds(16 * me, 16), :], place, sem_keep.at[2, chunk]).start()

    def arrive(chunk):
        bytes_of(xin.at[chunk, :, pl.ds(0, 448), :], sem_x.at[1, chunk])
        bytes_of(xin.at[chunk, :, pl.ds(0, 64), :], sem_keep.at[0, chunk])
        bytes_of(yin.at[chunk, pl.ds(0, 31)], sem_y.at[1, chunk])
        bytes_of(yin.at[chunk, 0], sem_keep.at[1, chunk])

    def gather(chunk):
        bytes_of(own.at[0, :, pl.ds(0, 31)], sem_p.at[1, chunk])
        bytes_of(own.at[0, :, 0], sem_keep.at[2, chunk])
        place = place_of(chunk)
        src = own.at[place]

        def to_partner(dst):
            remote(
                src, dst.at[place], sem_near.at[0, chunk], sem_near.at[1, chunk], across_rows(partner)
            ).start()

        @pl.when(is_kind(chunk, SHARED))
        def _():
            to_partner(own)

        @pl.when(jnp.logical_not(is_kind(chunk, SHARED)))
        def _():
            to_partner(nearby)

        @pl.when(is_inner)
        def _():
            remote(
                src, across.at[place], sem_across.at[0, chunk], sem_across.at[1, chunk], across_rows(other)
            ).start()

        @pl.when(is_outer & is_kind(chunk, SHARED))
        def _():
            remote(
                src, across.at[place], sem_far.at[0, chunk - 4], sem_far.at[1, chunk - 4], across_rows(far)
            ).start()

    def gather_last():
        chunk = CHUNKS - 1
        bytes_of(own.at[0, :, pl.ds(0, 31)], sem_p.at[1, chunk])
        bytes_of(own.at[0, :, 0], sem_keep.at[2, chunk])
        place = chunk + 2
        for p in range(2):
            remote(
                own.at[place, p],
                nearby.at[place, p],
                sem_near.at[0, chunk + p],
                sem_near.at[1, chunk + p],
                across_rows(partner),
            ).start()

            @pl.when(is_inner)
            def _():
                remote(
                    own.at[place, p],
                    across.at[place, p],
                    sem_across.at[0, chunk + p],
                    sem_across.at[1, chunk + p],
                    across_rows(other),
                ).start()

    def from_partner(chunk):
        bytes_of(own.at[0], sem_near.at[1, chunk])

    def from_other(chunk):
        bytes_of(own.at[0], sem_across.at[1, chunk])

    def turn(kind):
        def part(p, carry):
            def one(s, inside):
                square = jnp.concatenate([graw[kind, p, s], graw[kind, p, s + 16]], axis=0).astype(jnp.float32)
                swap[pl.ds(s, 128, stride=16), :] = square.T
                return inside

            lax.fori_loop(0, 16, one, 0, unroll=4)
            turned[kind, p] = swap[...].astype(jnp.bfloat16).reshape(32, 64, 128)
            return carry

        lax.fori_loop(0, 2, part, 0)

    lane = lax.broadcasted_iota(jnp.int32, (16, 128), 1)

    def correlate(chunk):
        for p in range(2):
            xcat[:, p * 128 : (p + 1) * 128] = xin[chunk, p]
        for p in range(2):
            for c in range(4):
                for k in range(4):
                    one = yin[chunk, c * 8 + 2 * k, p].astype(jnp.float32)
                    two = yin[chunk, c * 8 + 2 * k + 1, p].astype(jnp.float32)
                    first = jnp.where(lane < 64, one, pltpu.roll(two, 64, 1))
                    second = jnp.where(lane < 64, pltpu.roll(one, 64, 1), two)
                    base = p * 128 + c * 32
                    ycat[base : base + 16, k * 128 : (k + 1) * 128] = first.astype(jnp.bfloat16)
                    ycat[base + 16 : base + 32, k * 128 : (k + 1) * 128] = second.astype(jnp.bfloat16)
        spec_one[...] = jnp.dot(forward[...], xcat[...], preferred_element_type=jnp.float32)
        spec_two[...] = lax.dot_general(
            forward[...], ycat[...], (((1,), (1,)), ((), ())), preferred_element_type=jnp.float32
        )

        def mix(step, inner):
            cos_rows = pl.ds(step * 16, 16)
            sin_rows = pl.ds(FREQ + step * 16, 16)
            one_rr, one_ri = spec_one[cos_rows, 0:128], spec_one[cos_rows, 128:256]
            one_sr, one_si = spec_one[sin_rows, 0:128], spec_one[sin_rows, 128:256]
            two_rr, two_ri = spec_two[cos_rows, 0:128], spec_two[cos_rows, 128:256]
            two_sr, two_si = spec_two[sin_rows, 0:128], spec_two[sin_rows, 128:256]
            a_re, a_im = one_rr + one_si, one_ri - one_sr
            a_re_m, a_im_m = one_rr - one_si, one_ri + one_sr
            b_re, b_im = two_rr - two_si, two_ri + two_sr
            b_re_m, b_im_m = two_rr + two_si, two_ri - two_sr
            s_re = a_re * b_re - a_im * b_im
            s_im = a_re * b_im + a_im * b_re
            s_re_m = a_re_m * b_re_m - a_im_m * b_im_m
            s_im_m = a_re_m * b_im_m + a_im_m * b_re_m
            product[cos_rows, 0:128] = (s_re + s_re_m).astype(jnp.bfloat16)
            product[sin_rows, 0:128] = (s_im_m - s_im).astype(jnp.bfloat16)
            product[cos_rows, 128:256] = (s_im + s_im_m).astype(jnp.bfloat16)
            product[sin_rows, 128:256] = (s_re - s_re_m).astype(jnp.bfloat16)
            return inner

        lax.fori_loop(0, FREQ // 16, mix, 0, unroll=8)
        lagged = jnp.dot(inverse[...], product[...], preferred_element_type=jnp.float32)
        scale = 1.0 / (LENGTH * 32.0)
        pout[chunk, 0] = (scale * lagged[:, 128:256]).astype(jnp.bfloat16)
        pout[chunk, 1] = (-scale * lagged[:, 0:128]).astype(jnp.bfloat16)

    def apply_left(tiles, kind, side, column, parts=(0, 2)):
        def part(p, carry):
            swap[...] = tiles[pl.ds(4 * kind, 4), p].astype(jnp.float32).reshape(2048, 128)
            for pair in range(8):
                both = jnp.concatenate(
                    [
                        swap[pl.ds(2 * pair, 128, stride=16), :],
                        swap[pl.ds(2 * pair + 1, 128, stride=16), :],
                    ],
                    axis=1,
                ).astype(jnp.bfloat16)
                made = jnp.dot(left[side], both, preferred_element_type=jnp.float32)
                lower = pl.ds(256 * pair, 128)
                upper = pl.ds(256 * pair + 128, 128)
                total[p, column, lower, :] += made[:, 0:128]
                total[p, column, upper, :] += made[:, 128:256]
            return carry

        lax.fori_loop(*parts, part, 0)

    def finish_early(p, carry):
        def block(quad, inside):
            rows = pl.ds(quad * 512, 512)
            whole = jnp.concatenate([total[p, b, rows, :].astype(jnp.bfloat16) for b in range(5)], axis=1)
            for first, count, low, high in ((0, 2, 0, 384), (2, 2, 128, 640), (4, 1, 384, 640)):
                made = jnp.dot(
                    whole[:, low:high],
                    right[low:high, first * 128 : (first + count) * 128],
                    preferred_element_type=jnp.float32,
                )
                for s in range(first, first + count):
                    for lag in range(4):
                        wide[p, s, pl.ds(quad * 4 + lag, 128, stride=16), :] = made[
                            lag * 128 : lag * 128 + 128, (s - first) * 128 : (s - first) * 128 + 128
                        ]
            return inside

        lax.fori_loop(0, 4, block, 0)
        for s in range(5):

            @pl.when((s < last - 1) | (s > last + 1))
            def _():
                out[p, 0, s] = wide[p, s].astype(jnp.bfloat16).reshape(128, 16, 128)

        return carry

    def finish_last(p, carry):
        bytes_of(own.at[0, 0], sem_near.at[1, CHUNKS - 1 + p])

        @pl.when(is_inner)
        def _():
            bytes_of(own.at[0, 0], sem_across.at[1, CHUNKS - 1 + p])

        swap[...] = nearby[pl.ds(8, 4), p].astype(jnp.float32).reshape(2048, 128)
        swap_two[...] = across[pl.ds(8, 4), p].astype(jnp.float32).reshape(2048, 128)
        both_left = jnp.concatenate([left[1 + toward], left[1 + inward]], axis=1)
        for pair in range(8):
            both = jnp.concatenate(
                [
                    jnp.concatenate(
                        [
                            held[pl.ds(2 * pair, 128, stride=16), :],
                            held[pl.ds(2 * pair + 1, 128, stride=16), :],
                        ],
                        axis=1,
                    )
                    for held in (swap, swap_two)
                ],
                axis=0,
            ).astype(jnp.bfloat16)
            made = jnp.dot(both_left, both, preferred_element_type=jnp.float32)
            lower = pl.ds(256 * pair, 128)
            upper = pl.ds(256 * pair + 128, 128)
            mixed[pl.ds(2 * pair, 128, stride=16), :] = made[:, 0:128] + total[p, last, lower, :]
            mixed[pl.ds(2 * pair + 1, 128, stride=16), :] = made[:, 128:256] + total[p, last, upper, :]
        for near in range(3):
            s = last + near - 1

            @pl.when((s >= 0) & (s < 5))
            def _():
                made = jnp.dot(
                    mixed[...].astype(jnp.bfloat16), right_last[near], preferred_element_type=jnp.float32
                )
                out[p, 0, s] = (wide[p, s] + made).astype(jnp.bfloat16).reshape(128, 16, 128)

        return carry

    send_x(jnp.int32(0))
    send_x(jnp.int32(1))
    load_diag.wait()
    turn(DIAG)
    send_y(jnp.int32(0))
    send_y(jnp.int32(1))

    @pl.when(is_outer)
    def _():
        bytes_of(graw.at[SHARED], sem_load.at[3])
        turn(SHARED)
        pltpu.make_async_copy(turned.at[SHARED, :, :, pl.ds(0, 32), :], ypass, sem_load.at[5]).start()
        remote(
            turned.at[SHARED, :, :, pl.ds(32, 32), :], ypass, sem_pass.at[2], sem_pass.at[3], across_rows(partner)
        ).start()

    place = lax.broadcasted_iota(jnp.int32, (128, 128), 1)
    orbital = lax.broadcasted_iota(jnp.int32, (128, 128), 0)
    order = (orbital == 4 * lax.rem(place, 32) + place // 32).astype(jnp.bfloat16)
    for side in range(3):
        left[side] = jnp.dot(coupling[row, side], order, preferred_element_type=jnp.float32).astype(jnp.bfloat16)
    for b, s in ((2, 0), (1, 3), (4, 2)):
        right[b * 128 : b * 128 + 128, s * 128 : s * 128 + 128] = jnp.zeros((128, 128), jnp.bfloat16)
    for b in range(5):
        for s in range(max(b - 1, 0), min(b + 2, 5)):
            block = (slice(b * 128, b * 128 + 128), slice(s * 128, s * 128 + 128))
            tile_b, tile_c = row + b - 2, row + s - 2
            inside = (
                (tile_b >= 0) & (tile_b < 4) & (tile_c >= 0) & (tile_c < 4) & (b != last)
            ).astype(jnp.float32)
            safe = jnp.clip(tile_c, 0, 3)
            tile = coupling[safe, b - s + 1].astype(jnp.float32) * inside
            right[block] = tile.T.astype(jnp.bfloat16)

    for near in range(3):
        tile_b, tile_c = row + last - 2, row + last - 2 + near - 1
        inside = ((tile_c >= 0) & (tile_c < 4)).astype(jnp.float32)
        tile = coupling[jnp.clip(tile_c, 0, 3), 2 - near].astype(jnp.float32) * inside
        right_last[near] = tile.T.astype(jnp.bfloat16)

    @pl.when(is_outer)
    def _():
        for place in range(8, 12):
            across[place] = jnp.zeros((2, 32, 16, 128), jnp.bfloat16)

    def clear(step, carry):
        for b in range(5):
            total[0, b, pl.ds(step * 256, 256), :] = jnp.zeros((256, 128), jnp.float32)
            total[1, b, pl.ds(step * 256, 256), :] = jnp.zeros((256, 128), jnp.float32)
        return carry

    lax.fori_loop(0, 8, clear, 0)
    load_forward.wait()
    load_inverse.wait()


    def step(chunk, carry):
        arrive(chunk)
        ahead = chunk + AHEAD

        @pl.when(ahead < 4)
        def _():
            send_x(ahead)

        @pl.when((ahead > 6) & (ahead < CHUNKS))
        def _():
            send_x(ahead)

        correlate(chunk)
        send_p(chunk)

        @pl.when(ahead == 4)
        def _():
            @pl.when(is_outer)
            def _():
                bytes_of(xpass, sem_pass.at[1])
                bytes_of(ypass, sem_load.at[5])

            @pl.when(is_inner)
            def _():
                bytes_of(xpass, sem_load.at[4])
                bytes_of(ypass, sem_pass.at[3])

        @pl.when(ahead == 6)
        def _():
            bytes_of(graw.at[INWARD], sem_raw.at[2])
            turn(INWARD)

        @pl.when(ahead < CHUNKS)
        def _():
            @pl.when((ahead >= 4) & (ahead <= 6))
            def _():
                send_x(ahead)

            send_y(ahead)

        @pl.when(chunk >= 1)
        def _():
            gather(chunk - 1)

        @pl.when(chunk == 6)
        def _():
            apply_left(own, 0, 1, 2)

        @pl.when(chunk == 7)
        def _():
            for early in range(4):
                from_partner(early)
            apply_left(nearby, 0, 1 + toward, 2 + toward)

        @pl.when((chunk == 8) & is_inner)
        def _():
            for early in range(4):
                from_other(early)
            apply_left(across, 0, 1 + inward, 2 + inward)

        return carry

    lax.fori_loop(0, CHUNKS, step, 0)

    from_partner(4)
    from_partner(5)
    apply_left(own, 1, 1 + inward * (1 - inner), 2 - inward * inner)
    gather_last()
    apply_left(own, 2, 1, 2 + inward)

    @pl.when(is_inner)
    def _():
        for chunk in range(4, 6):
            from_other(chunk)
            bytes_of(own.at[0], sem_far.at[1, chunk - 4])
        apply_left(across, 1, 1 + inward, 2 + 2 * inward)

    lax.fori_loop(0, 2, finish_early, 0)
    for chunk in range(6, CHUNKS - 1):
        from_partner(chunk)

    @pl.when(is_inner)
    def _():
        for chunk in range(6, CHUNKS - 1):
            from_other(chunk)

    lax.fori_loop(0, 2, finish_last, 0)
    @pl.when(is_inner)
    def _():
        bytes_of(xpass, sem_pass.at[0])
        bytes_of(graw.at[INWARD], sem_raw.at[0])
        bytes_of(graw.at[INWARD], sem_raw.at[1])

    @pl.when(is_outer)
    def _():
        bytes_of(ypass, sem_pass.at[2])
        for chunk in range(4, 6):
            bytes_of(own.at[0], sem_far.at[0, chunk - 4])

    def sent(chunk, carry):
        bytes_of(xin.at[chunk, :, pl.ds(0, 448), :], sem_x.at[0, chunk])
        bytes_of(yin.at[chunk, pl.ds(0, 31)], sem_y.at[0, chunk])
        bytes_of(own.at[0, :, pl.ds(0, 31)], sem_p.at[0, chunk])
        return carry

    def passed_on(chunk, carry):
        bytes_of(own.at[0], sem_near.at[0, chunk])

        @pl.when(is_inner)
        def _():
            bytes_of(own.at[0], sem_across.at[0, chunk])

        return carry

    lax.fori_loop(0, CHUNKS, sent, 0)
    lax.fori_loop(0, CHUNKS - 1, passed_on, 0)
    for p in range(2):
        bytes_of(own.at[0, 0], sem_near.at[0, CHUNKS - 1 + p])

        @pl.when(is_inner)
        def _():
            bytes_of(own.at[0, 0], sem_across.at[0, CHUNKS - 1 + p])


def shards(lesser, greater, coupling):
    forward, inverse = tables(512)
    half = jnp.bfloat16
    whole = jnp.float32
    anywhere = pl.BlockSpec(memory_space=pl.ANY)
    return pl.pallas_call(
        kernel,
        out_shape=pltpu.VMEM((2, 1, 5, 128, 16, 128), half),
        in_specs=[anywhere, anywhere, pl.BlockSpec(memory_space=pltpu.VMEM), anywhere, anywhere],
        out_specs=pl.BlockSpec(memory_space=pltpu.VMEM),
        scratch_shapes=[
            pltpu.VMEM((LENGTH, 512), half),
            pltpu.VMEM((512, LENGTH), half),
            pltpu.VMEM((3, 2, 32, 64, 128), half),
            pltpu.VMEM((3, 2, 32, 64, 128), half),
            pltpu.VMEM((2, 8, 2, 64, 128), half),
            pltpu.VMEM((2, 32, 32, 128), half),
            pltpu.VMEM((CHUNKS, 2, 512, 128), half),
            pltpu.VMEM((CHUNKS, 32, 2, 16, 128), half),
            pltpu.VMEM((CHUNKS, 2, 512, 128), half),
            pltpu.VMEM((12, 2, 32, 16, 128), half),
            pltpu.VMEM((12, 2, 32, 16, 128), half),
            pltpu.VMEM((12, 2, 32, 16, 128), half),
            pltpu.VMEM((2, 5, 2048, 128), whole),
            pltpu.VMEM((2048, 128), whole),
            pltpu.VMEM((2048, 128), whole),
            pltpu.VMEM((2048, 128), whole),
            pltpu.VMEM((2, 5, 2048, 128), whole),
            pltpu.VMEM((3, 128, 128), half),
            pltpu.VMEM((640, 640), half),
            pltpu.VMEM((3, 128, 128), half),
            pltpu.VMEM((512, 256), half),
            pltpu.VMEM((256, 512), half),
            pltpu.VMEM((LENGTH, 256), whole),
            pltpu.VMEM((LENGTH, 256), whole),
            pltpu.VMEM((LENGTH, 256), half),
            pltpu.SemaphoreType.DMA((6,)),
            pltpu.SemaphoreType.DMA((3, CHUNKS)),
            pltpu.SemaphoreType.DMA((3,)),
            pltpu.SemaphoreType.DMA((4,)),
            pltpu.SemaphoreType.DMA((2, CHUNKS)),
            pltpu.SemaphoreType.DMA((2, CHUNKS)),
            pltpu.SemaphoreType.DMA((2, CHUNKS)),
            pltpu.SemaphoreType.DMA((2, CHUNKS + 1)),
            pltpu.SemaphoreType.DMA((2, CHUNKS + 1)),
            pltpu.SemaphoreType.DMA((2, 2)),
        ],
        compiler_params=pltpu.CompilerParams(
            collective_id=0, has_side_effects=True, vmem_limit_bytes=55 * 1024 * 1024
        ),
        cost_estimate=pl.CostEstimate(flops=10**10, bytes_accessed=2 * 10**7, transcendentals=0),
    )(
        lesser.reshape(2, 3, 8, 4, 64, 128),
        greater.reshape(2, 3, 32, 64, 128),
        coupling,
        jnp.asarray(forward),
        jnp.asarray(inverse),
    )


def solution(mesh):
    placed = (P(None, "row", None, "col", "en", None), P(None, "row", None, "col", "en", None), P())
    return jax.shard_map(
        shards,
        mesh=mesh,
        in_specs=placed,
        out_specs=P(None, "row", None, None, ("col", "en"), None),
        check_vma=False,
    )
```
